32 devices in a mesh: section: 2 (over x), dp: 4 (over z), tensor: 4 (over y, core).
Axes of the slice: x: 2, y: 2, z: 4, core: 2. Of those that a mesh axis runs over, the one named last changes fastest.
Arguments:
- section_input: bfloat16 [2, 4, 256, 4096], P('section', 'dp', 'tensor'), may hold values from -6 to 6
- carried_grad: bfloat16 [2, 4, 256, 4096], P('section', 'dp', 'tensor'), may hold values from -6 to 6
- hidden_grad: bfloat16 [2, 4, 256, 3584], P('section', 'dp', None, 'tensor'), may hold values from -6 to 6
- saved_gate: bfloat16 [2, 4, 256, 3584], P('section', 'dp', None, 'tensor'), may hold values from -8 to 8
- w_up: bfloat16 [2, 4096, 3584], P('section', 'dp', 'tensor'), may hold values from -0.09375 to 0.09375
Outputs:
- passed_grad: bfloat16 [2, 4, 256, 4096], P('section', 'dp', 'tensor')
- up_weight_grad: bfloat16 [2, 4096, 3584], P('section', 'dp', 'tensor')
The draws below stay inside these ranges and needn't reach their ends.
All inputs are finite; a program needn't handle non-finite values.
Results may differ from the reference program's by a relative error of at most 0.015.
Values may be sent and summed in bfloat16 or wider, within the bound.
No kernel may reach another device: no remote copies, remote signals or barrier semaphores. Data moves between devices by JAX's collectives and lax.ppermute only.
A program may use at most 64 MiB of HBM per device.

```python
import jax
import jax.numpy as jnp
from jax import lax

D = 4096
TOK = 256
FF = 3584
SECTIONS = 2
REPLICAS = 4
N_TENSOR = 4


def strengthened(result, rng, source, target, blocks, factor):
    owner, partner = [(jnp.arange(result.shape[position]) // (result.shape[position] // blocks)).reshape([-1 if axis == position else 1 for axis in range(result.ndim)]) for position in (source, target)]
    chosen = jax.random.permutation(rng, blocks)[partner]
    strong = (owner == chosen) | (owner == (partner + blocks // 2) % blocks)
    return jnp.where(strong, factor * result, result)


def steps_of(key, dims, pieces, least, top_value):
    loudness = 1.0
    for dim, shards_of in pieces:
        heights = jax.random.uniform(jax.random.fold_in(jax.random.fold_in(key, 6), dim), (shards_of,), jnp.float32, least / len(pieces), top_value / len(pieces))
        loudness = loudness * jnp.repeat(jnp.exp(heights), dims[dim] // shards_of).reshape((-1,) + (1,) * (len(dims) - 1 - dim))
    return loudness


def gaussian(key, shape, deviation, reach, pieces=(), held_as=jnp.bfloat16):
    factor_of = steps_of(key, shape, pieces, -0.22, 0.18) if pieces else 1.0
    entries = jax.random.normal(key, shape, jnp.float32) * deviation * factor_of
    return jnp.minimum(jnp.maximum(entries, -reach), reach).astype(held_as)


def gaussian_with(key, shape, deviation, most, cuts, heavy, dtype=jnp.bfloat16):
    drawn = deviation * jax.random.normal(key, shape, jnp.float32)
    if cuts:
        drawn = drawn * steps_of(key, shape, cuts, -0.22, 0.18)
    return jnp.clip(strengthened(drawn, jax.random.fold_in(key, 3), *heavy), -most, most).astype(dtype)


def setup_inputs(seed: int = 0) -> dict:
    streams_of = jax.random.split(jax.random.key(seed), 6)
    return {
        "section_input": gaussian(streams_of[0], (SECTIONS, REPLICAS, TOK, D), 1.0, 6.0, ((0, 2), (1, 4), (2, 4))),
        "carried_grad": gaussian(streams_of[1], (SECTIONS, REPLICAS, TOK, D), 1.0, 6.0, ((0, 2), (1, 4), (2, 4))),
        "hidden_grad": gaussian_with(streams_of[2], (SECTIONS, REPLICAS, TOK, FF), 1.0, 6.0, ((0, 2), (1, 4), (3, 4)), (3, 2, 4, 2.0)),
        "saved_gate": gaussian(streams_of[3], (SECTIONS, REPLICAS, TOK, FF), 1.5, 8.0, ((0, 2), (1, 4), (3, 4))),
        "w_up": gaussian(streams_of[4], (SECTIONS, D, FF), D ** -0.5, 0.09375, ((0, 2), (1, 4), (2, 4))),
    }


def section_backward(item):
    inputs, carried, grads, gates, up_weight = item
    width = up_weight.shape[0]

    def one_replica(rep):
        carried_rows, grad_rows, gate_rows = rep
        gate = gate_rows.astype(jnp.float32)
        sig = jax.nn.sigmoid(gate)
        up_grad = (grad_rows.astype(jnp.float32) * gate * sig).astype(jnp.bfloat16)
        tokens = up_grad.shape[0]
        up_blocks = up_grad.reshape(tokens, N_TENSOR, -1).astype(jnp.float32)
        weight_blocks = up_weight.reshape(width, N_TENSOR, -1).astype(jnp.float32)
        parts = jnp.einsum('tnf,dnf->ntd', up_blocks, weight_blocks)
        parts = lax.optimization_barrier(parts.astype(jnp.bfloat16)).astype(jnp.float32)
        input_grad = (jnp.sum(parts, axis=0) + carried_rows.astype(jnp.float32)).astype(jnp.bfloat16)
        return input_grad, up_grad

    input_grad, up_grad = lax.map(one_replica, (carried, grads, gates))
    weight_grad = jnp.dot(inputs.reshape(-1, width).T, up_grad.reshape(-1, up_grad.shape[-1]), preferred_element_type=jnp.float32)
    return input_grad, (weight_grad / inputs.shape[0]).astype(jnp.bfloat16)


def reference(section_input, carried_grad, hidden_grad, saved_gate, w_up):
    input_grad, up_weight_grad = lax.map(section_backward, (section_input, carried_grad, hidden_grad, saved_gate, w_up))
    passed_grad = jnp.concatenate([input_grad[1:], jnp.zeros_like(input_grad[:1])], axis=0)
    return passed_grad, up_weight_grad
```

```python
import jax
import jax.numpy as jnp
from jax import lax
from jax.sharding import PartitionSpec as P

AXES = ("section", "dp", "tensor")
BF16 = jnp.bfloat16
F32 = jnp.float32


def moved(value, sizes, target):
    sections, replicas, shards = sizes
    pairs = []
    for s in range(sections):
        for r in range(replicas):
            for t in range(shards):
                to = target(s, r, t)
                if to is not None:
                    source = (s * replicas + r) * shards + t
                    pairs.append((source, (to[0] * replicas + to[1]) * shards + to[2]))
    return lax.ppermute(value, AXES, pairs)


def after(value, *others):
    return lax.optimization_barrier((value, *others))[0]


def gathered(block, sizes, t):
    shards = sizes[2]
    step = shards // 2
    while step:
        other = moved(block, sizes, lambda s, r, i: (s, r, i ^ step))
        mine_first = (t & step) == 0
        a = block[None] if block.ndim == 2 else block
        b = other[None] if other.ndim == 2 else other
        first = jnp.where(mine_first, a, b)
        second = jnp.where(mine_first, b, a)
        block = jnp.stack([first, second], axis=1).reshape(-1, *a.shape[1:])
        step //= 2
    return block.reshape(-1, block.shape[-1])


def scattered(parts, sizes, t):
    shards = sizes[2]
    rows, columns = parts.shape
    value = parts.reshape(shards, rows // shards, columns)
    step = 1
    while step < shards:
        value = value.reshape(-1, 2, rows // shards, columns)
        bit = (t // step) & 1
        keep = lax.dynamic_index_in_dim(value, bit, 1, keepdims=False)
        give = lax.dynamic_index_in_dim(value, 1 - bit, 1, keepdims=False)
        got = moved(give, sizes, lambda s, r, i: (s, r, i ^ step) if s > 0 else None)
        value = (keep.astype(F32) + got.astype(F32)).astype(BF16)
        step *= 2
    return value.reshape(rows // shards, columns)


def body(section_input, carried_grad, hidden_grad, saved_gate, w_up):
    sizes = tuple(lax.axis_size(a) for a in AXES)
    sections, replicas, shards = sizes
    r, t = lax.axis_index("dp"), lax.axis_index("tensor")
    x = section_input[0, 0]
    w = w_up[0]
    width = w.shape[0]
    rows = x.shape[0]

    gate = saved_gate[0, 0].astype(F32)
    ug = (hidden_grad[0, 0].astype(F32) * gate * jax.nn.sigmoid(gate)).astype(BF16)

    carried = moved(carried_grad[0, 0], sizes, lambda s, i, j: (s - 1, i, j) if s > 0 else None)

    def x_columns(k):
        return lax.dynamic_slice(x, (0, ((r + k) % replicas) * width), (rows, width))

    def turned(value, k):
        return moved(value, sizes, lambda s, i, j: (s, (i + k) % replicas, j))

    ugs, xs, pieces = [ug], [x_columns(0)], []
    xs.append(turned(x_columns(1), 1))
    for k in range(1, replicas):
        ugs.append(turned(ugs[-1], 1))
    for k in range(2, replicas):
        xs.append(turned(after(x_columns(k), ugs[-1]), k))
    for k in range(replicas):
        part = lax.dot_general(ugs[k], w, (((1,), (1,)), ((), ())), preferred_element_type=F32).astype(BF16)
        piece = scattered(part, sizes, t)
        pieces.append(
            moved(piece, sizes, lambda s, i, j: (s - 1, (i - k) % replicas, j) if s > 0 else None)
        )
    total = 0
    for k in range(replicas):
        total = total + lax.dot_general(
            gathered(xs[k], sizes, t), ugs[k], (((0,), (0,)), ((), ())), preferred_element_type=F32
        )
    weight_grad = (total / replicas).astype(BF16)

    stacked = jnp.stack(pieces, axis=1)
    ordered = jnp.roll(stacked, r, axis=1).reshape(rows, -1)
    passed = (carried.astype(F32) + ordered.astype(F32)).astype(BF16)
    return passed[None, None], weight_grad[None]


def solution(mesh):
    return jax.shard_map(
        body,
        mesh=mesh,
        in_specs=(
            P("section", "dp", "tensor", None),
            P("section", "dp", "tensor", None),
            P("section", "dp", None, "tensor"),
            P("section", "dp", None, "tensor"),
            P("section", "dp", "tensor"),
        ),
        out_specs=(P("section", "dp", "tensor", None), P("section", "dp", "tensor")),
        check_vma=False,
    )
```

```python
import functools

import jax
import jax.numpy as jnp
from jax import lax
from jax.experimental import pallas as pl
from jax.experimental.pallas import tpu as pltpu
from jax.sharding import PartitionSpec as P

AXES = ("section", "dp", "tensor")
BF16 = jnp.bfloat16
F32 = jnp.float32
VMEM = pl.BlockSpec(memory_space=pltpu.VMEM)
HBM = pl.BlockSpec(memory_space=pltpu.HBM)
NT = (((1,), (1,)), ((), ()))
TN = (((0,), (0,)), ((), ()))
LANES = 128
START = 58


def moved(value, sizes, target):
    sections, replicas, shards = sizes
    pairs = []
    for s in range(sections):
        for r in range(replicas):
            for t in range(shards):
                to_s, to_r, to_t = target(s, r, t)
                pairs.append(
                    ((s * replicas + r) * shards + t, (to_s * replicas + to_r) * shards + to_t)
                )
    return lax.ppermute(value, AXES, pairs)


def together(*values):
    return lax.optimization_barrier(values)


def call(kernel, outputs, *arrays, limit=8, **more):
    options = dict(in_specs=[VMEM] * len(arrays), out_specs=[VMEM] * len(outputs))
    return pl.pallas_call(
        kernel,
        out_shape=[v if hasattr(v, "dtype") else jax.ShapeDtypeStruct(v, BF16) for v in outputs],
        compiler_params=pltpu.CompilerParams(vmem_limit_bytes=limit * 2**20),
        **{**options, **more},
    )(*arrays)


def added(a, b):
    return (a.astype(F32) + b.astype(F32)).astype(BF16)


def start_kernel(cut, shards, items, grad, gate, x, *refs):
    *outs, grad_here, gate_here, x_here, arrived, x_arrived = refs
    tokens, hidden = grad.shape
    replicas = len(x_here)
    width = x.shape[1] // replicas
    half = outs[0].shape[1]
    copies = []
    for shard in range(shards):
        here = pl.ds((2 * shard + cut) * half, half) if half % 16 == 0 else pl.ds(2 * shard * half, 2 * half)
        for i, (source, to) in enumerate(((grad, grad_here), (gate, gate_here))):
            copies.append(pltpu.make_async_copy(source.at[here], to.at[here], arrived.at[i, shard]))
            copies[-1].start()
    x_copies = {}
    for of in items:
        for device, _ in of:
            if device not in x_copies:
                block = lax.rem(lax.axis_index("dp") + device, replicas)
                columns = pl.ds(pl.multiple_of(block * width, width), width)
                x_copies[device] = pltpu.make_async_copy(x.at[:, columns], x_here[device], x_arrived.at[device])
                x_copies[device].start()
    at = outs[-1].shape[0] - hidden // LANES * shards
    for shard in range(shards):
        copies[2 * shard].wait()
        copies[2 * shard + 1].wait()
        here = pl.ds((2 * shard + cut) * half, half)
        for column in range(hidden // LANES):
            lanes = pl.ds(column * LANES, LANES)
            g = gate_here[here, lanes].astype(F32)
            value = grad_here[here, lanes].astype(F32) * g * (0.5 + 0.5 * jnp.tanh(0.5 * g))
            outs[-1][at + column * shards + shard] = value.astype(BF16)
    for copy in x_copies.values():
        copy.wait()
    for out, of in zip(outs, items):
        at = 0
        for device, cuts in of:
            for column in range(width // LANES):
                for c in cuts:
                    out[at] = x_here[device][c * half : (c + 1) * half, column * LANES : (column + 1) * LANES]
                    at += 1


def held_kernel(source, out, done):
    copy = pltpu.make_async_copy(source, out, done)
    copy.start()
    copy.wait()


def stack_kernel(places, *refs):
    *sources, out = refs
    for source, first, count, to, step in places:
        for i in range(count):
            out[to + i * step] = sources[source][first + i]


def product_kernel(shards, offsets, *refs):
    *pieces, w, keep, give = refs
    columns = w.shape[1] // LANES
    bit = lax.rem(lax.axis_index("tensor"), 2)
    left = [
        jnp.concatenate([piece[at + c * shards + 2 * m + start] for c in range(columns)], axis=1)
        for start in (bit, 1 - bit)
        for piece, at in zip(pieces, offsets)
        for m in range(shards // 2)
    ]
    out = lax.dot_general(jnp.concatenate(left), w[...], NT, preferred_element_type=F32).astype(BF16)
    rows = out.shape[0] // 2
    keep[...] = out[:rows].reshape(keep.shape)
    give[...] = out[rows:].reshape(give.shape)


def fold_kernel(step, *refs):
    *pairs, keep, give = refs
    bit = lax.rem(lax.div(lax.axis_index("tensor"), step), 2)
    at = 0
    for mine, got in zip(pairs[::2], pairs[1::2]):
        n, shards = mine.shape[:2]
        for i in range(n):
            for m in range(shards // 2):
                for to, start in ((keep, bit), (give, 1 - bit)):
                    to[at + i, m] = added(mine[i, 2 * m + start], got[i, 2 * m + start])
        at += n


def sum_kernel(mine, got, *outs):
    at = 0
    for out in outs:
        n = out.shape[0] // mine.shape[2]
        here = pl.ds(at, n)
        out[...] = added(mine[here], got[here]).reshape(out.shape)
        at += n


def weight_kernel(order, pairs, scale, xs, *refs):
    inputs, rest = refs[: 2 * xs], refs[2 * xs :]
    *rest, out, right = rest
    count = 1 + max(p[0] for p in pairs)
    parts, so_far = rest[:count], rest[count:]
    half = parts[0].shape[1]
    hidden = out.shape[1]
    shards = 2 * len(order)
    blocks = [(i, j, other) for other in (0, 1) for i, j in enumerate(order)]

    @pl.when(pl.program_id(0) == 0)
    def _():
        row = 0
        for part, at, _, _ in pairs:
            for _, j, other in blocks:
                shard = lax.axis_index("tensor") ^ j ^ other
                for c in range(hidden // LANES):
                    right[pl.ds(row, half), pl.ds(c * LANES, LANES)] = parts[part][at + c * shards + shard]
                row += half

    tile = out.shape[0]
    first = pl.program_id(0) * (tile // LANES)
    left = []
    for _, _, x, at in pairs:
        for i, _, other in blocks:
            block = inputs[2 * x + other]
            start = i * (block.shape[0] // len(order)) + at
            left.append(
                jnp.concatenate([block[start + 2 * (first + c)] for c in range(tile // LANES)], axis=1)
            )
    total = lax.dot_general(jnp.concatenate(left), right[...], TN, preferred_element_type=F32)
    for already in so_far:
        total += already[pl.ds(pl.multiple_of(pl.program_id(0) * tile, tile), tile)]
    out[...] = (total / scale).astype(out.dtype)


def passed_kernel(blocks, base, *refs):
    *pieces, out = refs
    width = pieces[0].shape[1]
    replicas = base.shape[1] // width
    sent = lax.axis_index("section") < lax.axis_size("section") - 1
    out[...] = jnp.where(sent, base[...], jnp.zeros(base.shape, BF16))
    for block, piece in zip(blocks, pieces):
        device = lax.rem(lax.axis_index("dp") + block, replicas)
        here = (slice(None), pl.ds(pl.multiple_of(device * width, width), width))
        out[here] = jnp.where(sent, added(base[here], piece[...]), jnp.zeros(piece.shape, BF16))


def last_kernel(base, piece, _, out, total, done):
    width = total.shape[1]
    replicas = base.shape[1] // width
    device = lax.rem(lax.axis_index("dp") + 1, replicas)
    columns = pl.ds(pl.multiple_of(device * width, width), width)
    sent = lax.axis_index("section") < lax.axis_size("section") - 1
    total[...] = jnp.where(sent, added(base[:, columns], piece[...]), jnp.zeros(piece.shape, BF16))
    copy = pltpu.make_async_copy(total, out.at[:, columns], done)
    copy.start()
    copy.wait()


def body(section_input, carried_grad, hidden_grad, saved_gate, w_up):
    sizes = tuple(lax.axis_size(a) for a in AXES)
    sections, replicas, shards = sizes
    grad, gate, x = hidden_grad[0, 0], saved_gate[0, 0], section_input[0, 0]
    w = w_up[0]
    width, hidden = w.shape
    tokens, rows = grad.shape[0], x.shape[0]
    half = rows // 2
    last, middle = replicas - 1, replicas // 2
    up_count, x_count = hidden // LANES * shards, width // LANES

    def up(value):
        return moved(value, sizes, lambda s, i, j: (s, (i + 1) % replicas, j))

    def down(value):
        return moved(value, sizes, lambda s, i, j: (s, (i - 1) % replicas, j))

    def returned(value, k):
        return moved(
            value,
            sizes,
            lambda s, i, j: (s - 1, (i - k) % replicas, j) if s else (sections - 1, i, j),
        )

    def across(value, step):
        return moved(value, sizes, lambda s, i, j: (s, i, j ^ step))

    def product(*pieces):
        share = (len(pieces), shards // 2, half, width)
        kernel = functools.partial(product_kernel, shards, [at for _, at in pieces])
        return call(kernel, [share, share], *[piece for piece, _ in pieces], w)

    def fold(step, *pairs):
        n, m = sum(v.shape[0] for v in pairs[::2]), pairs[0].shape[1]
        share = (n, m // 2, half, width)
        return call(functools.partial(fold_kernel, step), [share, share], *pairs)

    def finished(mine, got, *halves):
        step = 4
        while step < shards:
            mine, give = fold(step, mine, got)
            got = across(give, step)
            step *= 2
        return call(sum_kernel, [(n * half, width) for n in halves], mine, got)

    def stacked(count, places, *sources):
        return call(functools.partial(stack_kernel, places), [(count, half, LANES)], *sources)[0]

    def doubled(block, step, steps):
        for _ in range(steps):
            n = block.shape[0]
            places = [(i, 0, n, i * n, 1) for i in range(2)]
            block = stacked(2 * n, places, block, across(block, step))
            step //= 2
        return block

    far_step, steps = shards // 2, shards.bit_length() - 1
    order = [0]
    for i in range(steps - 1):
        order += [j + (far_step >> i) for j in order]

    def started(cut, *more):
        mine = [(d if cut == 0 else replicas - d, (0, 1)) for d in range(1, (replicas + 1) // 2)]
        if replicas % 2 == 0:
            mine.append((middle, (cut,)))
        items = [*more, mine]
        counts = [sum(x_count * len(cuts) for _, cuts in of) for of in items]
        counts[-1] += up_count
        return call(
            functools.partial(start_kernel, cut, shards, items),
            [(n, half, LANES) for n in counts],
            grad,
            gate,
            x,
            in_specs=[HBM] * 3,
            scratch_shapes=[pltpu.VMEM((tokens, hidden), BF16)] * 2
            + [[pltpu.VMEM((rows, width), BF16)] * replicas]
            + [pltpu.SemaphoreType.DMA((2, shards)), pltpu.SemaphoreType.DMA((replicas,))],
            limit=START,
        )

    tile = 256

    def weight_product(xs, pairs, parts, *so_far, final):
        kernel = functools.partial(weight_kernel, order, pairs, replicas if final else 1, len(xs))
        return call(
            kernel,
            [jax.ShapeDtypeStruct((width, hidden), BF16 if final else F32)],
            *[v for x in xs for v in x],
            *parts,
            *so_far,
            grid=(width // tile,),
            out_specs=[pl.BlockSpec((tile, hidden), lambda i: (i, 0))],
            scratch_shapes=[pltpu.VMEM((len(pairs) * shards * half, hidden), BF16)],
            limit=20,
        )[0]

    a = started(0)[0]
    a_next = up(a)
    x_own, b = started(1, [(0, (0, 1))])
    b_next = down(b)
    base = returned(carried_grad[0, 0], 0)
    w = call(held_kernel, [w.shape], w, in_specs=[HBM], scratch_shapes=[pltpu.SemaphoreType.DMA])[0]
    at = a.shape[0] - up_count
    a_parts, b_parts, ats = [a], [b], [at]
    keep, give = product((a, at), (b, at))
    keep, give = fold(2, keep, across(give, 1))
    out = finished(keep, across(give, 2), 2)[0]
    x_own = doubled(x_own, far_step, steps - 1)
    x_own = [x_own, across(x_own, 1)]

    a, b, base, out, *x_own = together(a_next, b_next, base, out, *x_own)
    a_parts.append(a)
    b_parts.append(b)
    ats.append(at)
    a_next, b_next = up(a[2 * x_count :]), down(b[2 * x_count :])
    zero = returned(out, 0)
    keep, give = product((a, at), (b, at))
    keep, give = fold(2, keep, across(give, 1))
    x_near = stacked(4 * x_count, [(i, 0, 2 * x_count, 2 * i * x_count, 1) for i in range(2)], a, b)
    x_near = doubled(x_near, far_step, steps - 1)

    at -= 2 * x_count
    a, b, keep, give, zero, x_near = together(a_next, b_next, keep, give, zero, x_near)
    a_parts.append(a)
    b_parts.append(b)
    ats.append(at)
    a_next, b_next = up(a[x_count:]), down(b[x_count:])
    nears = finished(keep, across(give, 2), 1, 1)
    keep, give = product((a, at), (b, at))
    keep, give = fold(2, keep, across(give, 1))
    x_far = stacked(2 * x_count, [(i, 0, x_count, i, 2) for i in range(2)], a, b)
    x_far = doubled(x_far, far_step, steps - 1)

    at -= x_count
    a, *nears = together(a_next, *nears)
    a_parts.append(a)
    ats.append(at)
    out = finished(keep, across(give, 2), 2)[0]
    keep_a, give_a = product((a, at))
    got_a = across(give_a, 1)
    b, keep_a, got_a, out, x_far = together(b_next, keep_a, got_a, out, x_far)
    b_parts.append(b)
    keep_b, give_b = product((b, at))
    x_near, x_far, give_b = together(x_near, x_far, give_b)
    keep, give = fold(2, keep_a, got_a, keep_b, across(give_b, 1))
    got = across(give, 2)
    out, _ = together(out, give)
    two = returned(out, 2)
    x_near, x_far = [x_near, across(x_near, 1)], [x_far, across(x_far, 1)]

    parts = [v for pair_of in zip(a_parts, b_parts) for v in pair_of]
    x_own[0], _ = together(x_own[0], give)
    weight_grad = weight_product(
        [x_own, x_near],
        [
            (0, ats[0], 0, 0),
            (1, ats[0], 0, 1),
            (2, ats[1], 1, 0),
            (3, ats[1], 1, 2 * x_count + 1),
        ],
        parts[:4],
        final=False,
    )
    keep, weight_grad = together(keep, weight_grad)
    out_a, out = finished(keep, got, 1, 1)
    above = returned(jnp.concatenate([out_a, nears[1]]), -1)
    below = returned(jnp.concatenate([nears[0], out]), 1)

    weight_grad, _ = together(weight_grad, out)
    weight_grad = weight_product(
        [x_near, x_far],
        [
            (0, ats[2], 1, 0),
            (1, ats[2], 1, 1),
            (2, ats[3], 0, 2 * x_count),
            (3, ats[3], 0, 1),
        ],
        parts[4:],
        weight_grad,
        final=True,
    )
    two, above, weight_grad = together(two, above, weight_grad)
    passed = call(
        functools.partial(passed_kernel, [0, 2, last]),
        [(rows, replicas * width)],
        base,
        zero,
        two,
        above,
    )[0]
    passed, below = together(passed, below)
    passed = call(
        last_kernel,
        [passed.shape],
        base,
        below,
        passed,
        in_specs=[VMEM] * 2 + [HBM],
        out_specs=[HBM],
        scratch_shapes=[pltpu.VMEM((rows, width), BF16), pltpu.SemaphoreType.DMA],
        input_output_aliases={2: 0},
    )[0]
    return passed[None, None], weight_grad[None]


def solution(mesh):
    return jax.shard_map(
        body,
        mesh=mesh,
        in_specs=(
            P("section", "dp", "tensor", None),
            P("section", "dp", "tensor", None),
            P("section", "dp", None, "tensor"),
            P("section", "dp", None, "tensor"),
            P("section", "dp", "tensor"),
        ),
        out_specs=(P("section", "dp", "tensor", None), P("section", "dp", "tensor")),
        check_vma=False,
    )
```

```python
import functools

import jax
import jax.numpy as jnp
from jax import lax
from jax.experimental import pallas as pl
from jax.experimental.pallas import tpu as pltpu
from jax.sharding import PartitionSpec as P

AXES = ("section", "dp", "tensor")
BF16 = jnp.bfloat16
F32 = jnp.float32
VMEM = pl.BlockSpec(memory_space=pltpu.VMEM)
HBM = pl.BlockSpec(memory_space=pltpu.HBM)
NT = (((1,), (1,)), ((), ()))
TN = (((0,), (0,)), ((), ()))
LANES = 128
START = 58


def moved(value, sizes, target):
    sections, replicas, shards = sizes
    pairs = []
    for s in range(sections):
        for r in range(replicas):
            for t in range(shards):
                to_s, to_r, to_t = target(s, r, t)
                pairs.append(
                    ((s * replicas + r) * shards + t, (to_s * replicas + to_r) * shards + to_t)
                )
    return lax.ppermute(value, AXES, pairs)


def together(*values):
    return lax.optimization_barrier(values)


def shifted(r, k, replicas):
    return lax.rem(r + k % replicas, replicas) if isinstance(r, jax.Array) else (r + k) % replicas


def call(kernel, outputs, *arrays, limit=8, flops=0, **more):
    size = sum(v.size * v.dtype.itemsize for v in arrays)
    if flops:
        more["cost_estimate"] = pl.CostEstimate(flops=flops, bytes_accessed=size, transcendentals=0)
    options = dict(in_specs=[VMEM] * len(arrays), out_specs=[VMEM] * len(outputs))
    return pl.pallas_call(
        kernel,
        out_shape=[v if hasattr(v, "dtype") else jax.ShapeDtypeStruct(v, BF16) for v in outputs],
        compiler_params=pltpu.CompilerParams(vmem_limit_bytes=limit * 2**20),
        **{**options, **more},
    )(*arrays)


def added(a, b):
    return (a.astype(F32) + b.astype(F32)).astype(BF16)


def start_kernel(shards, items, grad, gate, x, *refs):
    *outs, grad_here, gate_here, x_here, arrived, x_arrived = refs
    tokens, hidden = grad.shape
    replicas = len(x_here)
    width = x.shape[1] // replicas
    half = outs[0].shape[1]
    copies = []
    for shard in range(shards):
        here = pl.ds(2 * shard * half, 2 * half)
        for i, (source, to) in enumerate(((grad, grad_here), (gate, gate_here))):
            copies.append(pltpu.make_async_copy(source.at[here], to.at[here], arrived.at[i, shard]))
            copies[-1].start()
    x_copies = []
    for device in range(replicas):
        block = shifted(lax.axis_index("dp"), device, replicas)
        columns = pl.ds(pl.multiple_of(block * width, width), width)
        x_copies.append(pltpu.make_async_copy(x.at[:, columns], x_here[device], x_arrived.at[device]))
        x_copies[-1].start()
    for shard in range(shards):
        copies[2 * shard].wait()
        copies[2 * shard + 1].wait()
        for out, (_, cut) in zip(outs, items):
            if cut is None:
                continue
            at = out.shape[0] - hidden // LANES * shards + shard
            here = pl.ds((2 * shard + cut) * half, half)
            for column in range(hidden // LANES):
                lanes = pl.ds(column * LANES, LANES)
                g = gate_here[here, lanes].astype(F32)
                value = grad_here[here, lanes].astype(F32) * g * (0.5 + 0.5 * jnp.tanh(0.5 * g))
                out[at + column * shards] = value.astype(BF16)
    for copy in x_copies:
        copy.wait()
    for out, (of, _) in zip(outs, items):
        at = 0
        for device, cuts in of:
            for column in range(width // LANES):
                for c in cuts:
                    out[at] = x_here[device][c * half : (c + 1) * half, column * LANES : (column + 1) * LANES]
                    at += 1


def held_kernel(source, out, done):
    copy = pltpu.make_async_copy(source, out, done)
    copy.start()
    copy.wait()


def stack_kernel(places, *refs):
    *sources, out = refs
    for source, first, count, to, step in places:
        for i in range(count):
            out[to + i * step] = sources[source][first + i]


def product_kernel(shards, offsets, *refs):
    pieces, w, outs = refs[: len(offsets)], refs[len(offsets)], refs[len(offsets) + 1 :]
    columns = w.shape[1] // LANES
    bit = lax.rem(lax.axis_index("tensor"), 2)
    left = [
        jnp.concatenate([piece[at + c * shards + 2 * m + start] for c in range(columns)], axis=1)
        for start in (bit, 1 - bit)
        for piece, at in zip(pieces, offsets)
        for m in range(shards // 2)
    ]
    out = lax.dot_general(jnp.concatenate(left), w[...], NT, preferred_element_type=F32).astype(BF16)
    rows = out.shape[0] // 2
    for i, (mine, theirs) in enumerate(zip(outs[::2], outs[1::2])):
        n = rows // (len(outs) // 2)
        mine[...] = out[i * n : (i + 1) * n].reshape(mine.shape)
        theirs[...] = out[rows + i * n : rows + (i + 1) * n].reshape(theirs.shape)


def dealt_kernel(shards, offsets, rider, riders, *refs):
    pieces, w, outs = refs[: len(offsets)], refs[len(offsets)], refs[len(offsets) + 1 :]
    columns = w.shape[1] // LANES
    left = [
        jnp.concatenate([piece[at + c * shards + (lax.axis_index("tensor") ^ j)] for c in range(columns)], axis=1)
        for j in range(shards)
        for piece, at in zip(pieces, offsets)
    ]
    total = lax.dot_general(jnp.concatenate(left), w[...], NT, preferred_element_type=F32).astype(BF16)
    rows = total.shape[0] // shards
    for j, out in enumerate(outs):
        if j != rider:
            out[...] = total[j * rows : (j + 1) * rows]
            continue
        half = out.shape[1]
        for n in range(rows // half):
            for c in range(total.shape[1] // LANES):
                out[c * (rows // half) + n] = total[
                    j * rows + n * half : j * rows + (n + 1) * half, c * LANES : (c + 1) * LANES
                ]
        for piece, first, count, to, step in riders:
            for i in range(count):
                out[rows // half * (total.shape[1] // LANES) + to + i * step] = pieces[piece][first + i]


def total_kernel(count, rider, *refs):
    parts, outs = refs[:count], refs[count:]
    rows, width = parts[0].shape
    total = sum(part[...].astype(F32) for j, part in enumerate(parts) if j != rider)
    at = 0
    for out in outs:
        value = total[at : at + out.shape[0]]
        if rider is not None:
            packed = parts[rider]
            half = packed.shape[1]
            blocks = [
                jnp.concatenate(
                    [packed[c * (rows // half) + n] for c in range(width // LANES)], axis=1
                )
                for n in range(at // half, (at + out.shape[0]) // half)
            ]
            value = value + jnp.concatenate(blocks).astype(F32)
        out[...] = value.astype(BF16)
        at += out.shape[0]


def fold_kernel(step, *refs):
    *pairs, keep, give = refs
    bit = lax.rem(lax.div(lax.axis_index("tensor"), step), 2)
    at = 0
    for mine, got in zip(pairs[::2], pairs[1::2]):
        n, shards = mine.shape[:2]
        for i in range(n):
            for m in range(shards // 2):
                for to, start in ((keep, bit), (give, 1 - bit)):
                    to[at + i, m] = added(mine[i, 2 * m + start], got[i, 2 * m + start])
        at += n


def sum_kernel(mine, got, *outs):
    at = 0
    for out in outs:
        n = out.shape[0] // mine.shape[2]
        here = pl.ds(at, n)
        out[...] = added(mine[here], got[here]).reshape(out.shape)
        at += n


def weight_kernel(order, pairs, scale, xs, *refs):
    inputs, rest = refs[: 2 * xs], refs[2 * xs :]
    *rest, out, right = rest
    count = 1 + max(p[0] for p in pairs)
    parts, so_far = rest[:count], rest[count:]
    half = parts[0].shape[1]
    hidden = out.shape[1]
    shards = 2 * len(order)
    blocks = [(i, j, other) for other in (0, 1) for i, j in enumerate(order)]

    @pl.when(pl.program_id(0) == 0)
    def _():
        row = 0
        for part, at, _, _ in pairs:
            for _, j, other in blocks:
                shard = lax.axis_index("tensor") ^ j ^ other
                for c in range(hidden // LANES):
                    right[pl.ds(row, half), pl.ds(c * LANES, LANES)] = parts[part][at + c * shards + shard]
                row += half

    tile = out.shape[0]
    first = pl.program_id(0) * (tile // LANES)
    left = []
    for _, _, x, at in pairs:
        for i, _, other in blocks:
            block = inputs[2 * x + other]
            start = i * (block.shape[0] // len(order)) + at
            left.append(
                jnp.concatenate([block[start + 2 * (first + c)] for c in range(tile // LANES)], axis=1)
            )
    total = lax.dot_general(jnp.concatenate(left), right[...], TN, preferred_element_type=F32)
    for already in so_far:
        total += already[pl.ds(pl.multiple_of(pl.program_id(0) * tile, tile), tile)]
    out[...] = (total / scale).astype(out.dtype)


def passed_kernel(blocks, base, *refs):
    *pieces, out = refs
    width = pieces[0].shape[1]
    replicas = base.shape[1] // width
    sent = lax.axis_index("section") < lax.axis_size("section") - 1
    out[...] = jnp.where(sent, base[...], jnp.zeros(base.shape, BF16))
    for block, piece in zip(blocks, pieces):
        device = shifted(lax.axis_index("dp"), block, replicas)
        here = (slice(None), pl.ds(pl.multiple_of(device * width, width), width))
        out[here] = jnp.where(sent, added(base[here], piece[...]), jnp.zeros(piece.shape, BF16))


def last_kernel(blocks, base, *refs):
    *pieces, _, out, total, done = refs
    width = pieces[0].shape[1]
    replicas = base.shape[1] // width
    sent = lax.axis_index("section") < lax.axis_size("section") - 1
    copies = []
    for i, (block, piece) in enumerate(zip(blocks, pieces)):
        device = shifted(lax.axis_index("dp"), block, replicas)
        columns = pl.ds(pl.multiple_of(device * width, width), width)
        total[i] = jnp.where(sent, added(base[:, columns], piece[...]), jnp.zeros(piece.shape, BF16))
        copies.append(pltpu.make_async_copy(total.at[i], out.at[:, columns], done.at[i]))
        copies[-1].start()
    for copy in copies:
        copy.wait()


def body(section_input, carried_grad, hidden_grad, saved_gate, w_up):
    sizes = tuple(lax.axis_size(a) for a in AXES)
    sections, replicas, shards = sizes
    grad, gate, x = hidden_grad[0, 0], saved_gate[0, 0], section_input[0, 0]
    w = w_up[0]
    width, hidden = w.shape
    tokens, rows = grad.shape[0], x.shape[0]
    half = rows // 2
    last, middle = replicas - 1, replicas // 2
    up_count, x_count = hidden // LANES * shards, width // LANES

    def up(value):
        return moved(value, sizes, lambda s, i, j: (s, shifted(i, 1, replicas), j))

    def down(value):
        return moved(value, sizes, lambda s, i, j: (s, shifted(i, -1, replicas), j))

    def returned(value, k):
        return moved(
            value,
            sizes,
            lambda s, i, j: (s - 1, shifted(i, -k, replicas), j) if s else (sections - 1, i, j),
        )

    def across(value, step):
        return moved(value, sizes, lambda s, i, j: (s, i, j ^ step))

    def product(*pieces, groups=1, flops=0):
        share = (len(pieces) // groups, shards // 2, half, width)
        kernel = functools.partial(product_kernel, shards, [at for _, at in pieces])
        return call(kernel, [share] * (2 * groups), *[piece for piece, _ in pieces], w, flops=flops)

    def summed(pieces, halves, rider=None, riders=()):
        kernel = functools.partial(dealt_kernel, shards, [at for _, at in pieces], rider, riders)
        shares = [(len(pieces) * half, width)] * shards
        own = len(pieces) * x_count
        if rider is not None:
            shares[rider] = (own + sum(count for _, _, count, _, _ in riders), half, LANES)
        mine, *others = call(kernel, shares, *[piece for piece, _ in pieces], w)
        others = [across(v, j + 1) for j, v in enumerate(others)]
        kernel = functools.partial(total_kernel, shards, rider)
        outs = call(kernel, [(n * half, width) for n in halves], mine, *others)
        return outs, others[rider - 1] if rider is not None else None

    def fold(step, *pairs):
        n, m = sum(v.shape[0] for v in pairs[::2]), pairs[0].shape[1]
        share = (n, m // 2, half, width)
        return call(functools.partial(fold_kernel, step), [share, share], *pairs)

    def finished(mine, got, *halves):
        step = 4
        while step < shards:
            mine, give = fold(step, mine, got)
            got = across(give, step)
            step *= 2
        return call(sum_kernel, [(n * half, width) for n in halves], mine, got)

    def stacked(count, places, *sources):
        return call(functools.partial(stack_kernel, places), [(count, half, LANES)], *sources)[0]

    def doubled(block, step, steps):
        for _ in range(steps):
            n = block.shape[0]
            places = [(i, 0, n, i * n, 1) for i in range(2)]
            block = stacked(2 * n, places, block, across(block, step))
            step //= 2
        return block

    far_step, steps = shards // 2, shards.bit_length() - 1
    order = [0]
    for i in range(steps - 1):
        order += [j + (far_step >> i) for j in order]

    tile = 256

    def weight_product(xs, pairs, parts, *so_far, final):
        kernel = functools.partial(weight_kernel, order, pairs, replicas if final else 1, len(xs))
        return call(
            kernel,
            [jax.ShapeDtypeStruct((width, hidden), BF16 if final else F32)],
            *[v for x in xs for v in x],
            *parts,
            *so_far,
            grid=(width // tile,),
            out_specs=[pl.BlockSpec((tile, hidden), lambda i: (i, 0))],
            scratch_shapes=[pltpu.VMEM((len(pairs) * shards * half, hidden), BF16)],
            limit=20,
        )[0]

    both = (0, 1)
    items = [[(d, both) for d in range(1, (replicas + 1) // 2)], [(last + 1 - d, both) for d in range(1, (replicas + 1) // 2)]]
    if replicas % 2 == 0:
        for cut in both:
            items[cut].append((middle, (cut,)))
    items = [(items[0], 0), (items[1], 1), ([(0, both)], None)]
    counts = [sum(x_count * len(cuts) for _, cuts in of) + (cut is not None) * up_count for of, cut in items]
    a, b, x_own = call(
        functools.partial(start_kernel, shards, items),
        [(n, half, LANES) for n in counts],
        grad,
        gate,
        x,
        in_specs=[HBM] * 3,
        scratch_shapes=[pltpu.VMEM((tokens, hidden), BF16)] * 2
        + [[pltpu.VMEM((rows, width), BF16)] * replicas]
        + [pltpu.SemaphoreType.DMA((2, shards)), pltpu.SemaphoreType.DMA((replicas,))],
        limit=START,
    )
    a_next, b_next = up(a), down(b)
    base = returned(carried_grad[0, 0], 0)
    w = call(held_kernel, [w.shape], w, in_specs=[HBM], scratch_shapes=[pltpu.SemaphoreType.DMA])[0]
    at = a.shape[0] - up_count
    a_parts, b_parts, ats = [a], [b], [at]
    (out,), _ = summed([(a, at), (b, at)], [2])
    x_own = doubled(x_own, far_step, steps - 1)
    x_own = [x_own, across(x_own, 1)]

    a, b, base, out, *x_own = together(a_next, b_next, base, out, *x_own)
    a_parts.append(a)
    b_parts.append(b)
    ats.append(at)
    a_next, b_next = up(a[2 * x_count :]), down(b[2 * x_count :])
    zero = returned(out, 0)
    keep_a, give_a, keep_b, give_b = product((a, at), (b, at), groups=2)
    keep, give = fold(2, keep_a, across(give_a, 1), keep_b, across(give_b, 1))
    nears = finished(keep, across(give, 2), 1, 1)
    x_near = stacked(4 * x_count, [(i, 0, 2 * x_count, 2 * i * x_count, 1) for i in range(2)], a, b)
    x_near = doubled(x_near, far_step, steps - 1)

    at -= 2 * x_count
    a, b, zero, *nears = together(a_next, b_next, zero, *nears)
    a_parts.append(a)
    b_parts.append(b)
    ats.append(at)
    a_next, b_next = up(a[x_count:]), down(b[x_count:])
    far_a, far_b, x_near = together(a, b, x_near)
    riders = [(i, 0, x_count, i, 2) for i in range(2)]
    (out,), x_far = summed([(far_a, at), (far_b, at)], [2], far_step, riders)

    at -= x_count
    a, b = a_next, b_next
    a_parts.append(a)
    b_parts.append(b)
    ats.append(at)
    keep, give = product((a, at), (b, at), flops=2 * tokens * hidden * width)
    x_far, give, out = together(x_far, give, out)
    two = returned(out, 0)
    keep, give = fold(2, keep, across(give, 1))
    got = across(give, 2)
    x_near = [x_near, across(x_near, 1)]
    places = [(i, 0, x_count, i, 2) for i in range(2)] + [(2, 2 * x_count, 2 * x_count, 2 * x_count, 1)]
    x_far = stacked(4 * x_count, places, a_parts[2], b_parts[2], x_far)
    x_far = doubled(x_far, far_step // 2, steps - 2)
    x_far = [x_far, across(x_far, 1)]

    parts = [v for pair_of in zip(a_parts, b_parts) for v in pair_of]
    x_own[0], _ = together(x_own[0], give)
    weight_grad = weight_product(
        [x_own, x_near],
        [
            (0, ats[0], 0, 0),
            (1, ats[0], 0, 1),
            (2, ats[1], 1, 0),
            (3, ats[1], 1, 2 * x_count + 1),
        ],
        parts[:4],
        final=False,
    )
    keep, got, two, weight_grad = together(keep, got, two, weight_grad)
    two = moved(
        two, sizes, lambda s, i, j: (s, shifted(i, -2, replicas), j) if s < sections - 1 else (s, i, j ^ 1)
    )
    out_a, out = finished(keep, got, 1, 1)
    above = returned(jnp.concatenate([out_a, nears[1]]), -1)
    below = returned(jnp.concatenate([nears[0], out]), 1)

    weight_grad, _ = together(weight_grad, out)
    weight_grad = weight_product(
        [x_near, x_far],
        [
            (0, ats[2], 1, 0),
            (1, ats[2], 1, 1),
            (2, ats[3], 0, 2 * x_count),
            (3, ats[3], 0, 1),
        ],
        parts[4:],
        weight_grad,
        final=True,
    )
    two, weight_grad = together(two, weight_grad)
    kernel = functools.partial(passed_kernel, [0, 2])
    passed = call(kernel, [(rows, replicas * width)], base, zero, two)[0]
    passed, above, below = together(passed, above, below)
    passed = call(
        functools.partial(last_kernel, [last, 1]),
        [passed.shape],
        base,
        above,
        below,
        passed,
        in_specs=[VMEM] * 3 + [HBM],
        out_specs=[HBM],
        scratch_shapes=[pltpu.VMEM((2, rows, width), BF16), pltpu.SemaphoreType.DMA((2,))],
        input_output_aliases={3: 0},
    )[0]
    return passed[None, None], weight_grad[None]


def solution(mesh):
    return jax.shard_map(
        body,
        mesh=mesh,
        in_specs=(
            P("section", "dp", "tensor", None),
            P("section", "dp", "tensor", None),
            P("section", "dp", None, "tensor"),
            P("section", "dp", None, "tensor"),
            P("section", "dp", "tensor"),
        ),
        out_specs=(P("section", "dp", "tensor", None), P("section", "dp", "tensor")),
        check_vma=False,
    )
```

```python
import functools

import jax
import jax.numpy as jnp
from jax import lax
from jax.experimental import pallas as pl
from jax.experimental.pallas import tpu as pltpu
from jax.sharding import PartitionSpec as P

AXES = ("section", "dp", "tensor")
BF16 = jnp.bfloat16
F32 = jnp.float32
VMEM = pl.BlockSpec(memory_space=pltpu.VMEM)
HBM = pl.BlockSpec(memory_space=pltpu.HBM)
NT = (((1,), (1,)), ((), ()))
TN = (((0,), (0,)), ((), ()))
LANES = 128
START = 53


def moved(value, sizes, target):
    sections, replicas, shards = sizes
    pairs = []
    for s in range(sections):
        for r in range(replicas):
            for t in range(shards):
                to_s, to_r, to_t = target(s, r, t)
                pairs.append(
                    ((s * replicas + r) * shards + t, (to_s * replicas + to_r) * shards + to_t)
                )
    return lax.ppermute(value, AXES, pairs)


def together(*values):
    return lax.optimization_barrier(values)


def shifted(r, k, replicas):
    if replicas != 4:
        return lax.rem(r + k % replicas, replicas) if isinstance(r, jax.Array) else (r + k) % replicas
    place = ((r ^ (r >> 1)) + k % 4) & 3
    return place ^ (place >> 1)


def call(kernel, outputs, *arrays, limit=8, flops=0, **more):
    size = sum(v.size * v.dtype.itemsize for v in arrays)
    if flops:
        more["cost_estimate"] = pl.CostEstimate(flops=flops, bytes_accessed=size, transcendentals=0)
    options = dict(in_specs=[VMEM] * len(arrays), out_specs=[VMEM] * len(outputs))
    return pl.pallas_call(
        kernel,
        out_shape=[v if hasattr(v, "dtype") else jax.ShapeDtypeStruct(v, BF16) for v in outputs],
        compiler_params=pltpu.CompilerParams(vmem_limit_bytes=limit * 2**20),
        **{**options, **more},
    )(*arrays)


def added(a, b):
    return (a.astype(F32) + b.astype(F32)).astype(BF16)


def start_kernel(shards, items, grad, gate, x, *refs):
    *outs, grad_here, gate_here, x_here, arrived, x_arrived = refs
    tokens, hidden = grad.shape
    replicas = len(x_here)
    width = x.shape[1] // replicas
    half = outs[0].shape[1]
    copies = []
    for shard in range(shards):
        here = pl.ds(2 * shard * half, 2 * half)
        for i, (source, to) in enumerate(((grad, grad_here), (gate, gate_here))):
            copies.append(pltpu.make_async_copy(source.at[here], to.at[here], arrived.at[i, shard]))
            copies[-1].start()
    x_copies = []
    for device in range(replicas):
        block = shifted(lax.axis_index("dp"), device, replicas)
        columns = pl.ds(pl.multiple_of(block * width, width), width)
        x_copies.append(pltpu.make_async_copy(x.at[:, columns], x_here[device], x_arrived.at[device]))
        x_copies[-1].start()
    for shard in range(shards):
        copies[2 * shard].wait()
        copies[2 * shard + 1].wait()
        for out, (_, cut) in zip(outs, items):
            if cut is None:
                continue
            at = out.shape[0] - hidden // LANES * shards + shard
            here = pl.ds((2 * shard + cut) * half, half)
            for column in range(hidden // LANES):
                lanes = pl.ds(column * LANES, LANES)
                g = gate_here[here, lanes].astype(F32)
                value = grad_here[here, lanes].astype(F32) * g * (0.5 + 0.5 * jnp.tanh(0.5 * g))
                out[at + column * shards] = value.astype(BF16)
    for copy in x_copies:
        copy.wait()
    for out, (of, _) in zip(outs, items):
        at = 0
        for device, cuts in of:
            for column in range(width // LANES):
                for c in cuts:
                    out[at] = x_here[device][c * half : (c + 1) * half, column * LANES : (column + 1) * LANES]
                    at += 1


def held_kernel(source, out, done):
    copy = pltpu.make_async_copy(source, out, done)
    copy.start()
    copy.wait()


def stack_kernel(places, *refs):
    *sources, out = refs
    for source, first, count, to, step in places:
        for i in range(count):
            out[to + i * step] = sources[source][first + i]


def product_kernel(shards, offsets, *refs):
    pieces, w, outs = refs[: len(offsets)], refs[len(offsets)], refs[len(offsets) + 1 :]
    columns = w.shape[1] // LANES
    bit = lax.rem(lax.axis_index("tensor"), 2)
    left = [
        jnp.concatenate([piece[at + c * shards + 2 * m + start] for c in range(columns)], axis=1)
        for start in (bit, 1 - bit)
        for piece, at in zip(pieces, offsets)
        for m in range(shards // 2)
    ]
    out = lax.dot_general(jnp.concatenate(left), w[...], NT, preferred_element_type=F32).astype(BF16)
    rows = out.shape[0] // 2
    for i, (mine, theirs) in enumerate(zip(outs[::2], outs[1::2])):
        n = rows // (len(outs) // 2)
        mine[...] = out[i * n : (i + 1) * n].reshape(mine.shape)
        theirs[...] = out[rows + i * n : rows + (i + 1) * n].reshape(theirs.shape)


def dealt_kernel(shards, offsets, rider, riders, *refs):
    pieces, w, outs = refs[: len(offsets)], refs[len(offsets)], refs[len(offsets) + 1 :]
    columns = w.shape[1] // LANES
    left = [
        jnp.concatenate([piece[at + c * shards + (lax.axis_index("tensor") ^ j)] for c in range(columns)], axis=1)
        for j in range(shards)
        for piece, at in zip(pieces, offsets)
    ]
    total = lax.dot_general(jnp.concatenate(left), w[...], NT, preferred_element_type=F32).astype(BF16)
    rows = total.shape[0] // shards
    for j, out in enumerate(outs):
        if j != rider:
            out[...] = total[j * rows : (j + 1) * rows]
            continue
        half = out.shape[1]
        for n in range(rows // half):
            for c in range(total.shape[1] // LANES):
                out[c * (rows // half) + n] = total[
                    j * rows + n * half : j * rows + (n + 1) * half, c * LANES : (c + 1) * LANES
                ]
        for piece, first, count, to, step in riders:
            for i in range(count):
                out[rows // half * (total.shape[1] // LANES) + to + i * step] = pieces[piece][first + i]


def total_kernel(count, rider, *refs):
    parts, outs = refs[:count], refs[count:]
    rows, width = parts[0].shape
    total = sum(part[...].astype(F32) for j, part in enumerate(parts) if j != rider)
    at = 0
    for out in outs:
        value = total[at : at + out.shape[0]]
        if rider is not None:
            packed = parts[rider]
            half = packed.shape[1]
            blocks = [
                jnp.concatenate(
                    [packed[c * (rows // half) + n] for c in range(width // LANES)], axis=1
                )
                for n in range(at // half, (at + out.shape[0]) // half)
            ]
            value = value + jnp.concatenate(blocks).astype(F32)
        out[...] = value.astype(BF16)
        at += out.shape[0]


def fold_kernel(step, *refs):
    *pairs, keep, give = refs
    bit = lax.rem(lax.div(lax.axis_index("tensor"), step), 2)
    at = 0
    for mine, got in zip(pairs[::2], pairs[1::2]):
        n, shards = mine.shape[:2]
        for i in range(n):
            for m in range(shards // 2):
                for to, start in ((keep, bit), (give, 1 - bit)):
                    to[at + i, m] = added(mine[i, 2 * m + start], got[i, 2 * m + start])
        at += n


def sum_kernel(mine, got, *outs):
    at = 0
    for out in outs:
        n = out.shape[0] // mine.shape[2]
        here = pl.ds(at, n)
        out[...] = added(mine[here], got[here]).reshape(out.shape)
        at += n


def weight_kernel(order, pairs, scale, xs, *refs):
    inputs, rest = refs[: 2 * xs], refs[2 * xs :]
    *rest, out, right = rest
    count = 1 + max(p[0] for p in pairs)
    parts, so_far = rest[:count], rest[count:]
    half = parts[0].shape[1]
    hidden = out.shape[1]
    shards = 2 * len(order)
    blocks = [(i, j, other) for other in (0, 1) for i, j in enumerate(order)]

    @pl.when(pl.program_id(0) == 0)
    def _():
        row = 0
        for part, at, _, _ in pairs:
            for _, j, other in blocks:
                shard = lax.axis_index("tensor") ^ j ^ other
                for c in range(hidden // LANES):
                    right[pl.ds(row, half), pl.ds(c * LANES, LANES)] = parts[part][at + c * shards + shard]
                row += half

    tile = out.shape[0]
    first = pl.program_id(0) * (tile // LANES)
    left = []
    for _, _, x, at in pairs:
        for i, _, other in blocks:
            block = inputs[2 * x + other]
            start = i * (block.shape[0] // len(order)) + at
            left.append(
                jnp.concatenate([block[start + 2 * (first + c)] for c in range(tile // LANES)], axis=1)
            )
    total = lax.dot_general(jnp.concatenate(left), right[...], TN, preferred_element_type=F32)
    for already in so_far:
        total += already[pl.ds(pl.multiple_of(pl.program_id(0) * tile, tile), tile)]
    out[...] = (total / scale).astype(out.dtype)


def passed_kernel(base, piece, out):
    width = piece.shape[1]
    sent = lax.axis_index("section") < lax.axis_size("section") - 1
    out[...] = jnp.where(sent, base[...], jnp.zeros(base.shape, BF16))
    here = (slice(None), pl.ds(pl.multiple_of(lax.axis_index("dp") * width, width), width))
    out[here] = jnp.where(sent, added(base[here], piece[...]), jnp.zeros(piece.shape, BF16))


def last_kernel(blocks, base, *refs):
    *pieces, _, out, total, done = refs
    width = pieces[0].shape[1]
    replicas = base.shape[1] // width
    sent = lax.axis_index("section") < lax.axis_size("section") - 1
    copies = []
    for i, (block, piece) in enumerate(zip(blocks, pieces)):
        device = shifted(lax.axis_index("dp"), block, replicas)
        columns = pl.ds(pl.multiple_of(device * width, width), width)
        total[i] = jnp.where(sent, added(base[:, columns], piece[...]), jnp.zeros(piece.shape, BF16))
        copies.append(pltpu.make_async_copy(total.at[i], out.at[:, columns], done.at[i]))
        copies[-1].start()
    for copy in copies:
        copy.wait()


def body(section_input, carried_grad, hidden_grad, saved_gate, w_up):
    sizes = tuple(lax.axis_size(a) for a in AXES)
    sections, replicas, shards = sizes
    grad, gate, x = hidden_grad[0, 0], saved_gate[0, 0], section_input[0, 0]
    w = w_up[0]
    width, hidden = w.shape
    tokens, rows = grad.shape[0], x.shape[0]
    half = rows // 2
    last, middle = replicas - 1, replicas // 2
    up_count, x_count = hidden // LANES * shards, width // LANES

    def up(value):
        return moved(value, sizes, lambda s, i, j: (s, shifted(i, 1, replicas), j))

    def down(value):
        return moved(value, sizes, lambda s, i, j: (s, shifted(i, -1, replicas), j))

    def returned(value, k):
        return moved(
            value,
            sizes,
            lambda s, i, j: (s - 1, shifted(i, -k, replicas), j) if s else (sections - 1, i, j),
        )

    def across(value, step):
        return moved(value, sizes, lambda s, i, j: (s, i, j ^ step))

    def product(*pieces, groups=1, flops=0):
        share = (len(pieces) // groups, shards // 2, half, width)
        kernel = functools.partial(product_kernel, shards, [at for _, at in pieces])
        return call(kernel, [share] * (2 * groups), *[piece for piece, _ in pieces], w, flops=flops)

    def summed(pieces, halves, rider=None, riders=()):
        kernel = functools.partial(dealt_kernel, shards, [at for _, at in pieces], rider, riders)
        shares = [(len(pieces) * half, width)] * shards
        own = len(pieces) * x_count
        if rider is not None:
            shares[rider] = (own + sum(count for _, _, count, _, _ in riders), half, LANES)
        mine, *others = call(kernel, shares, *[piece for piece, _ in pieces], w)
        others = [across(v, j + 1) for j, v in enumerate(others)]
        kernel = functools.partial(total_kernel, shards, rider)
        outs = call(kernel, [(n * half, width) for n in halves], mine, *others)
        return outs, others[rider - 1] if rider is not None else None

    def fold(step, *pairs):
        n, m = sum(v.shape[0] for v in pairs[::2]), pairs[0].shape[1]
        share = (n, m // 2, half, width)
        return call(functools.partial(fold_kernel, step), [share, share], *pairs)

    def finished(mine, got, *halves):
        step = 4
        while step < shards:
            mine, give = fold(step, mine, got)
            got = across(give, step)
            step *= 2
        return call(sum_kernel, [(n * half, width) for n in halves], mine, got)

    def stacked(count, places, *sources):
        return call(functools.partial(stack_kernel, places), [(count, half, LANES)], *sources)[0]

    def doubled(block, step, steps):
        for _ in range(steps):
            n = block.shape[0]
            places = [(i, 0, n, i * n, 1) for i in range(2)]
            block = stacked(2 * n, places, block, across(block, step))
            step //= 2
        return block

    far_step, steps = shards // 2, shards.bit_length() - 1
    order = [0]
    for i in range(steps - 1):
        order += [j + (far_step >> i) for j in order]

    tile = 256

    def weight_product(xs, pairs, parts, *so_far, final):
        kernel = functools.partial(weight_kernel, order, pairs, replicas if final else 1, len(xs))
        return call(
            kernel,
            [jax.ShapeDtypeStruct((width, hidden), BF16 if final else F32)],
            *[v for x in xs for v in x],
            *parts,
            *so_far,
            grid=(width // tile,),
            out_specs=[pl.BlockSpec((tile, hidden), lambda i: (i, 0))],
            scratch_shapes=[pltpu.VMEM((len(pairs) * shards * half, hidden), BF16)],
            limit=20,
        )[0]

    both = (0, 1)
    items = [[(d, both) for d in range(1, (replicas + 1) // 2)], [(last + 1 - d, both) for d in range(1, (replicas + 1) // 2)]]
    if replicas % 2 == 0:
        for cut in both:
            items[cut].append((middle, (cut,)))
    items = [(items[0], 0), (items[1], 1), ([(0, both)], None)]
    counts = [sum(x_count * len(cuts) for _, cuts in of) + (cut is not None) * up_count for of, cut in items]
    a, b, x_own = call(
        functools.partial(start_kernel, shards, items),
        [(n, half, LANES) for n in counts],
        grad,
        gate,
        x,
        in_specs=[HBM] * 3,
        scratch_shapes=[pltpu.VMEM((tokens, hidden), BF16)] * 2
        + [[pltpu.VMEM((rows, width), BF16)] * replicas]
        + [pltpu.SemaphoreType.DMA((2, shards)), pltpu.SemaphoreType.DMA((replicas,))],
        limit=START,
    )
    a_next, b_next = up(a), down(b)
    carried, *_ = together(carried_grad[0, 0], a, b)
    base = returned(carried, 0)
    w = call(held_kernel, [w.shape], w, in_specs=[HBM], scratch_shapes=[pltpu.SemaphoreType.DMA])[0]
    at = a.shape[0] - up_count
    a_parts, b_parts, ats = [a], [b], [at]
    (out,), _ = summed([(a, at), (b, at)], [2])
    x_own = doubled(x_own, far_step, steps - 1)
    x_own = [x_own, across(x_own, 1)]

    a, b, base, out, *x_own = together(a_next, b_next, base, out, *x_own)
    a_parts.append(a)
    b_parts.append(b)
    ats.append(at)
    a_next, b_next = up(a[2 * x_count :]), down(b[2 * x_count :])
    zero = returned(out, 0)
    keep_a, give_a, keep_b, give_b = product((a, at), (b, at), groups=2)
    keep, give = fold(2, keep_a, across(give_a, 1), keep_b, across(give_b, 1))
    nears = finished(keep, across(give, 2), 1, 1)
    x_near = stacked(4 * x_count, [(i, 0, 2 * x_count, 2 * i * x_count, 1) for i in range(2)], a, b)
    x_near = doubled(x_near, far_step, steps - 1)

    at -= 2 * x_count
    weight_grad = weight_product(
        [x_own], [(0, ats[0], 0, 0), (1, ats[0], 0, 1)], [a_parts[0], b_parts[0]], final=False
    )
    a, b, zero, weight_grad, *nears = together(a_next, b_next, zero, weight_grad, *nears)
    a_parts.append(a)
    b_parts.append(b)
    ats.append(at)
    a_next, b_next = up(a[x_count:]), down(b[x_count:])
    far_a, far_b, x_near = together(a, b, x_near)
    riders = [(i, 0, x_count, i, 2) for i in range(2)]
    (out,), x_far = summed([(far_a, at), (far_b, at)], [2], far_step, riders)

    at -= x_count
    a, b = a_next, b_next
    a_parts.append(a)
    b_parts.append(b)
    ats.append(at)
    keep, give = product((a, at), (b, at), flops=2 * tokens * hidden * width)
    passed = call(passed_kernel, [(rows, replicas * width)], base, zero)[0]
    x_far, give, out, passed = together(x_far, give, out, passed)
    two = returned(out, 0)
    keep, give = fold(2, keep, across(give, 1))
    got = across(give, 2)
    x_near = [x_near, across(x_near, 1)]
    places = [(i, 0, x_count, i, 2) for i in range(2)] + [(2, 2 * x_count, 2 * x_count, 2 * x_count, 1)]
    x_far = stacked(4 * x_count, places, a_parts[2], b_parts[2], x_far)
    x_far = doubled(x_far, far_step // 2, steps - 2)
    x_far = [x_far, across(x_far, 1)]

    parts = [v for pair_of in zip(a_parts, b_parts) for v in pair_of]
    keep, got, two = together(keep, got, two)
    two = moved(
        two, sizes, lambda s, i, j: (s, shifted(i, -2, replicas), j) if s < sections - 1 else (s, i, j ^ 1)
    )
    out_a, out = finished(keep, got, 1, 1)
    above = returned(jnp.concatenate([out_a, nears[1]]), -1)
    below = returned(jnp.concatenate([nears[0], out]), 1)

    weight_grad, _ = together(weight_grad, out)
    weight_grad = weight_product(
        [x_near, x_far],
        [
            (0, ats[1], 0, 0),
            (1, ats[1], 0, 2 * x_count + 1),
            (2, ats[2], 1, 0),
            (3, ats[2], 1, 1),
            (4, ats[3], 0, 2 * x_count),
            (5, ats[3], 0, 1),
        ],
        parts[2:],
        weight_grad,
        final=True,
    )
    passed, weight_grad = together(passed, weight_grad)
    passed = call(
        functools.partial(last_kernel, [2, last, 1]),
        [passed.shape],
        base,
        two,
        above,
        below,
        passed,
        in_specs=[VMEM] * 4 + [HBM],
        out_specs=[HBM],
        scratch_shapes=[pltpu.VMEM((3, rows, width), BF16), pltpu.SemaphoreType.DMA((3,))],
        input_output_aliases={4: 0},
    )[0]
    return passed[None, None], weight_grad[None]


def solution(mesh):
    return jax.shard_map(
        body,
        mesh=mesh,
        in_specs=(
            P("section", "dp", "tensor", None),
            P("section", "dp", "tensor", None),
            P("section", "dp", None, "tensor"),
            P("section", "dp", None, "tensor"),
            P("section", "dp", "tensor"),
        ),
        out_specs=(P("section", "dp", "tensor", None), P("section", "dp", "tensor")),
        check_vma=False,
    )
```

```python
import functools

import jax
import jax.numpy as jnp
from jax import lax
from jax.experimental import pallas as pl
from jax.experimental.pallas import tpu as pltpu
from jax.sharding import PartitionSpec as P

AXES = ("section", "dp", "tensor")
BF16 = jnp.bfloat16
F32 = jnp.float32
VMEM = pl.BlockSpec(memory_space=pltpu.VMEM)
HBM = pl.BlockSpec(memory_space=pltpu.HBM)
NT = (((1,), (1,)), ((), ()))
TN = (((0,), (0,)), ((), ()))
LANES = 128
START = 53


def moved(value, sizes, target):
    sections, replicas, shards = sizes
    pairs = []
    for s in range(sections):
        for r in range(replicas):
            for t in range(shards):
                to_s, to_r, to_t = target(s, r, t)
                pairs.append(
                    ((s * replicas + r) * shards + t, (to_s * replicas + to_r) * shards + to_t)
                )
    return lax.ppermute(value, AXES, pairs)


def together(*values):
    return lax.optimization_barrier(values)


def shifted(r, k, replicas):
    if replicas != 4:
        return lax.rem(r + k % replicas, replicas) if isinstance(r, jax.Array) else (r + k) % replicas
    place = ((r ^ (r >> 1)) + k % 4) & 3
    return place ^ (place >> 1)


def call(kernel, outputs, *arrays, limit=8, flops=0, **more):
    size = sum(v.size * v.dtype.itemsize for v in arrays)
    if flops:
        more["cost_estimate"] = pl.CostEstimate(flops=flops, bytes_accessed=size, transcendentals=0)
    options = dict(in_specs=[VMEM] * len(arrays), out_specs=[VMEM] * len(outputs))
    return pl.pallas_call(
        kernel,
        out_shape=[v if hasattr(v, "dtype") else jax.ShapeDtypeStruct(v, BF16) for v in outputs],
        compiler_params=pltpu.CompilerParams(vmem_limit_bytes=limit * 2**20),
        **{**options, **more},
    )(*arrays)


def added(a, b):
    return (a.astype(F32) + b.astype(F32)).astype(BF16)


def start_kernel(shards, items, grad, gate, x, *refs):
    *outs, grad_here, gate_here, x_here, arrived, x_arrived = refs
    tokens, hidden = grad.shape
    replicas = len(x_here)
    width = x.shape[1] // replicas
    half = outs[0].shape[1]
    copies = []
    for shard in range(shards):
        here = pl.ds(2 * shard * half, 2 * half)
        for i, (source, to) in enumerate(((grad, grad_here), (gate, gate_here))):
            copies.append(pltpu.make_async_copy(source.at[here], to.at[here], arrived.at[i, shard]))
            copies[-1].start()
    x_copies = []
    for device in range(replicas):
        block = shifted(lax.axis_index("dp"), device, replicas)
        columns = pl.ds(pl.multiple_of(block * width, width), width)
        x_copies.append(pltpu.make_async_copy(x.at[:, columns], x_here[device], x_arrived.at[device]))
        x_copies[-1].start()
    for shard in range(shards):
        copies[2 * shard].wait()
        copies[2 * shard + 1].wait()
        for out, (_, cut) in zip(outs, items):
            if cut is None:
                continue
            at = out.shape[0] - hidden // LANES * shards + shard
            here = pl.ds((2 * shard + cut) * half, half)
            for column in range(hidden // LANES):
                lanes = pl.ds(column * LANES, LANES)
                g = gate_here[here, lanes].astype(F32)
                value = grad_here[here, lanes].astype(F32) * g * (0.5 + 0.5 * jnp.tanh(0.5 * g))
                out[at + column * shards] = value.astype(BF16)
    for copy in x_copies:
        copy.wait()
    for out, (of, _) in zip(outs, items):
        at = 0
        for device, cuts in of:
            for column in range(width // LANES):
                for c in cuts:
                    out[at] = x_here[device][c * half : (c + 1) * half, column * LANES : (column + 1) * LANES]
                    at += 1


def held_kernel(source, out, done):
    copy = pltpu.make_async_copy(source, out, done)
    copy.start()
    copy.wait()


def stack_kernel(places, *refs):
    *sources, out = refs
    for source, first, count, to, step in places:
        for i in range(count):
            out[to + i * step] = sources[source][first + i]


def product_kernel(shards, offsets, *refs):
    pieces, w, outs = refs[: len(offsets)], refs[len(offsets)], refs[len(offsets) + 1 :]
    columns = w.shape[1] // LANES
    bit = lax.rem(lax.axis_index("tensor"), 2)
    left = [
        jnp.concatenate([piece[at + c * shards + 2 * m + start] for c in range(columns)], axis=1)
        for start in (bit, 1 - bit)
        for piece, at in zip(pieces, offsets)
        for m in range(shards // 2)
    ]
    out = lax.dot_general(jnp.concatenate(left), w[...], NT, preferred_element_type=F32).astype(BF16)
    rows = out.shape[0] // 2
    for i, (mine, theirs) in enumerate(zip(outs[::2], outs[1::2])):
        n = rows // (len(outs) // 2)
        mine[...] = out[i * n : (i + 1) * n].reshape(mine.shape)
        theirs[...] = out[rows + i * n : rows + (i + 1) * n].reshape(theirs.shape)


def dealt_kernel(shards, offsets, rider, riders, *refs):
    pieces, w, outs = refs[: len(offsets)], refs[len(offsets)], refs[len(offsets) + 1 :]
    columns = w.shape[1] // LANES
    left = [
        jnp.concatenate([piece[at + c * shards + (lax.axis_index("tensor") ^ j)] for c in range(columns)], axis=1)
        for j in range(shards)
        for piece, at in zip(pieces, offsets)
    ]
    total = lax.dot_general(jnp.concatenate(left), w[...], NT, preferred_element_type=F32).astype(BF16)
    rows = total.shape[0] // shards
    for j, out in enumerate(outs):
        if j != rider:
            out[...] = total[j * rows : (j + 1) * rows]
            continue
        half = out.shape[1]
        for n in range(rows // half):
            for c in range(total.shape[1] // LANES):
                out[c * (rows // half) + n] = total[
                    j * rows + n * half : j * rows + (n + 1) * half, c * LANES : (c + 1) * LANES
                ]
        for piece, first, count, to, step in riders:
            for i in range(count):
                out[rows // half * (total.shape[1] // LANES) + to + i * step] = pieces[piece][first + i]


def total_kernel(count, rider, *refs):
    parts, outs = refs[:count], refs[count:]
    rows, width = parts[0].shape
    total = sum(part[...].astype(F32) for j, part in enumerate(parts) if j != rider)
    at = 0
    for out in outs:
        value = total[at : at + out.shape[0]]
        if rider is not None:
            packed = parts[rider]
            half = packed.shape[1]
            blocks = [
                jnp.concatenate(
                    [packed[c * (rows // half) + n] for c in range(width // LANES)], axis=1
                )
                for n in range(at // half, (at + out.shape[0]) // half)
            ]
            value = value + jnp.concatenate(blocks).astype(F32)
        out[...] = value.astype(BF16)
        at += out.shape[0]


def fold_kernel(step, *refs):
    *pairs, keep, give = refs
    bit = lax.rem(lax.div(lax.axis_index("tensor"), step), 2)
    at = 0
    for mine, got in zip(pairs[::2], pairs[1::2]):
        n, shards = mine.shape[:2]
        for i in range(n):
            for m in range(shards // 2):
                for to, start in ((keep, bit), (give, 1 - bit)):
                    to[at + i, m] = added(mine[i, 2 * m + start], got[i, 2 * m + start])
        at += n


def sum_kernel(mine, got, *outs):
    at = 0
    for out in outs:
        n = out.shape[0] // mine.shape[2]
        here = pl.ds(at, n)
        out[...] = added(mine[here], got[here]).reshape(out.shape)
        at += n


def crossed_kernel(mine, got, first, second, above, below):
    half = first.shape[0]
    total = added(mine[...], got[...]).reshape(-1, first.shape[1])
    above[:half], above[half:] = total[:half], second[...]
    below[:half], below[half:] = first[...], total[half:]


def weight_kernel(groups, pairs, scale, count, *refs):
    inputs, rest = refs[:count], refs[count:]
    *rest, out, right = rest
    many = 1 + max(p[0] for p in pairs)
    parts, so_far = rest[:many], rest[many:]
    half = parts[0].shape[1]
    hidden = out.shape[1]
    shards = len(groups[0])

    @pl.when(pl.program_id(0) == 0)
    def _():
        row = 0
        for part, at, _, _ in pairs:
            for j in range(shards):
                shard = lax.axis_index("tensor") ^ j
                for c in range(hidden // LANES):
                    right[pl.ds(row, half), pl.ds(c * LANES, LANES)] = parts[part][at + c * shards + shard]
                row += half

    tile = out.shape[0]
    first = pl.program_id(0) * (tile // LANES)
    left = []
    for _, _, group, at in pairs:
        for j in range(shards):
            block, start = groups[group][j]
            columns = [inputs[block][start + at + 2 * (first + c)] for c in range(tile // LANES)]
            left.append(jnp.concatenate(columns, axis=1))
    total = lax.dot_general(jnp.concatenate(left), right[...], TN, preferred_element_type=F32)
    for already in so_far:
        total += already[pl.ds(pl.multiple_of(pl.program_id(0) * tile, tile), tile)]
    out[...] = (total / scale).astype(out.dtype)


def passed_kernel(base, piece, out):
    width = piece.shape[1]
    sent = lax.axis_index("section") < lax.axis_size("section") - 1
    out[...] = jnp.where(sent, base[...], jnp.zeros(base.shape, BF16))
    here = (slice(None), pl.ds(pl.multiple_of(lax.axis_index("dp") * width, width), width))
    out[here] = jnp.where(sent, added(base[here], piece[...]), jnp.zeros(piece.shape, BF16))


def last_kernel(blocks, base, *refs):
    *pieces, _, out, total, done = refs
    width = pieces[0].shape[1]
    replicas = base.shape[1] // width
    sent = lax.axis_index("section") < lax.axis_size("section") - 1
    copies = []
    for i, (block, piece) in enumerate(zip(blocks, pieces)):
        device = shifted(lax.axis_index("dp"), block, replicas)
        columns = pl.ds(pl.multiple_of(device * width, width), width)
        total[i] = jnp.where(sent, added(base[:, columns], piece[...]), jnp.zeros(piece.shape, BF16))
        copies.append(pltpu.make_async_copy(total.at[i], out.at[:, columns], done.at[i]))
        copies[-1].start()
    for copy in copies:
        copy.wait()


def body(section_input, carried_grad, hidden_grad, saved_gate, w_up):
    sizes = tuple(lax.axis_size(a) for a in AXES)
    sections, replicas, shards = sizes
    grad, gate, x = hidden_grad[0, 0], saved_gate[0, 0], section_input[0, 0]
    w = w_up[0]
    width, hidden = w.shape
    tokens, rows = grad.shape[0], x.shape[0]
    half = rows // 2
    last, middle = replicas - 1, replicas // 2
    up_count, x_count = hidden // LANES * shards, width // LANES

    def up(value):
        return moved(value, sizes, lambda s, i, j: (s, shifted(i, 1, replicas), j))

    def down(value):
        return moved(value, sizes, lambda s, i, j: (s, shifted(i, -1, replicas), j))

    def returned(value, k):
        return moved(
            value,
            sizes,
            lambda s, i, j: (s - 1, shifted(i, -k, replicas), j) if s else (sections - 1, i, j),
        )

    def across(value, step):
        return moved(value, sizes, lambda s, i, j: (s, i, j ^ step))

    def product(*pieces, groups=1, flops=0):
        share = (len(pieces) // groups, shards // 2, half, width)
        kernel = functools.partial(product_kernel, shards, [at for _, at in pieces])
        return call(kernel, [share] * (2 * groups), *[piece for piece, _ in pieces], w, flops=flops)

    def summed(pieces, halves, rider=None, riders=()):
        kernel = functools.partial(dealt_kernel, shards, [at for _, at in pieces], rider, riders)
        shares = [(len(pieces) * half, width)] * shards
        own = len(pieces) * x_count
        if rider is not None:
            shares[rider] = (own + sum(count for _, _, count, _, _ in riders), half, LANES)
        mine, *others = call(kernel, shares, *[piece for piece, _ in pieces], w)
        others = [across(v, j + 1) for j, v in enumerate(others)]
        kernel = functools.partial(total_kernel, shards, rider)
        outs = call(kernel, [(n * half, width) for n in halves], mine, *others)
        return outs, others[rider - 1] if rider is not None else None

    def fold(step, *pairs):
        n, m = sum(v.shape[0] for v in pairs[::2]), pairs[0].shape[1]
        share = (n, m // 2, half, width)
        return call(functools.partial(fold_kernel, step), [share, share], *pairs)

    def finished(mine, got, *halves):
        step = 4
        while step < shards:
            mine, give = fold(step, mine, got)
            got = across(give, step)
            step *= 2
        return call(sum_kernel, [(n * half, width) for n in halves], mine, got)

    def stacked(count, places, *sources):
        return call(functools.partial(stack_kernel, places), [(count, half, LANES)], *sources)[0]

    def doubled(block, step, steps):
        for _ in range(steps):
            n = block.shape[0]
            places = [(i, 0, n, i * n, 1) for i in range(2)]
            block = stacked(2 * n, places, block, across(block, step))
            step //= 2
        return block

    far_step, steps = shards // 2, shards.bit_length() - 1
    order = [0]
    for i in range(steps - 1):
        order += [j + (far_step >> i) for j in order]

    tile = 256

    def weight_product(xs, pairs, parts, *so_far, final):
        groups, at = [], 0
        for x in xs:
            group = [None] * shards
            for i, j in enumerate(order):
                for other in (0, 1):
                    if len(x) == 2:
                        group[j ^ other] = (at + other, i * (x[0].shape[0] // len(order)))
                    else:
                        group[j ^ other] = (at + (j ^ other), 0)
            groups.append(group)
            at += len(x)
        kernel = functools.partial(weight_kernel, groups, pairs, replicas if final else 1, at)
        return call(
            kernel,
            [jax.ShapeDtypeStruct((width, hidden), BF16 if final else F32)],
            *[v for x in xs for v in x],
            *parts,
            *so_far,
            grid=(width // tile,),
            out_specs=[pl.BlockSpec((tile, hidden), lambda i: (i, 0))],
            scratch_shapes=[pltpu.VMEM((len(pairs) * shards * half, hidden), BF16)],
            limit=20,
        )[0]

    both = (0, 1)
    items = [[(d, both) for d in range(1, (replicas + 1) // 2)], [(last + 1 - d, both) for d in range(1, (replicas + 1) // 2)]]
    if replicas % 2 == 0:
        for cut in both:
            items[cut].append((middle, (cut,)))
    items = [(items[0], 0), (items[1], 1), ([(0, both)], None)]
    counts = [sum(x_count * len(cuts) for _, cuts in of) + (cut is not None) * up_count for of, cut in items]
    a, b, x_own = call(
        functools.partial(start_kernel, shards, items),
        [(n, half, LANES) for n in counts],
        grad,
        gate,
        x,
        in_specs=[HBM] * 3,
        scratch_shapes=[pltpu.VMEM((tokens, hidden), BF16)] * 2
        + [[pltpu.VMEM((rows, width), BF16)] * replicas]
        + [pltpu.SemaphoreType.DMA((2, shards)), pltpu.SemaphoreType.DMA((replicas,))],
        limit=START,
    )
    a_next, b_next = up(a), down(b)
    carried, *_ = together(carried_grad[0, 0], a, b)
    base = returned(carried, 0)
    w = call(held_kernel, [w.shape], w, in_specs=[HBM], scratch_shapes=[pltpu.SemaphoreType.DMA])[0]
    at = a.shape[0] - up_count
    a_parts, b_parts, ats = [a], [b], [at]
    (out,), _ = summed([(a, at), (b, at)], [2])
    x_own = doubled(x_own, far_step, steps - 1)
    x_own = [x_own, across(x_own, 1)]

    a, b, base, out, *x_own = together(a_next, b_next, base, out, *x_own)
    a_parts.append(a)
    b_parts.append(b)
    ats.append(at)
    a_next, b_next = up(a[2 * x_count :]), down(b[2 * x_count :])
    zero = returned(out, 0)
    keep_a, give_a, keep_b, give_b = product((a, at), (b, at), groups=2)
    keep, give = fold(2, keep_a, across(give_a, 1), keep_b, across(give_b, 1))
    nears = finished(keep, across(give, 2), 1, 1)
    x_near = stacked(4 * x_count, [(i, 0, 2 * x_count, 2 * i * x_count, 1) for i in range(2)], a, b)
    x_near, step = {0: x_near}, far_step
    while step > 1:
        x_near |= {j + step: across(v, step) for j, v in x_near.items()}
        step //= 2
    blocks = sorted(x_near)
    x_near = [x_near[j] for j in blocks]

    at -= 2 * x_count
    weight_grad = weight_product(
        [x_own], [(0, ats[0], 0, 0), (1, ats[0], 0, 1)], [a_parts[0], b_parts[0]], final=False
    )
    a, b, zero, weight_grad, *nears = together(a_next, b_next, zero, weight_grad, *nears)
    a_parts.append(a)
    b_parts.append(b)
    ats.append(at)
    a_next, b_next = up(a[x_count:]), down(b[x_count:])
    far_a, far_b, *x_near = together(a, b, *x_near)
    riders = [(i, 0, x_count, i, 2) for i in range(2)]
    (out,), x_far = summed([(far_a, at), (far_b, at)], [2], far_step, riders)

    at -= x_count
    a, b = a_next, b_next
    a_parts.append(a)
    b_parts.append(b)
    ats.append(at)
    keep, give = product((a, at), (b, at), flops=2 * tokens * hidden * width)
    passed = call(passed_kernel, [(rows, replicas * width)], base, zero)[0]
    x_far, give, out, passed = together(x_far, give, out, passed)
    two = returned(out, 0)
    keep, give = fold(2, keep, across(give, 1))
    got = across(give, 2)
    x_near = [v for pair in ((v, across(v, 1)) for v in x_near) for v in pair]
    places = [(i, 0, x_count, i, 2) for i in range(2)] + [(2, 2 * x_count, 2 * x_count, 2 * x_count, 1)]
    x_far = stacked(4 * x_count, places, a_parts[2], b_parts[2], x_far)
    x_far = doubled(x_far, far_step // 2, steps - 2)
    x_far = [x_far, across(x_far, 1)]

    parts = [v for pair_of in zip(a_parts, b_parts) for v in pair_of]
    keep, got, two = together(keep, got, two)
    step = 4
    while step < shards:
        keep, give = fold(step, keep, got)
        got = across(give, step)
        step *= 2
    above, below = call(crossed_kernel, [(rows, width)] * 2, keep, got, *nears)
    out = above
    above, below = returned(above, -1), returned(below, 1)
    two = moved(
        two, sizes, lambda s, i, j: (s, shifted(i, -2, replicas), j) if s < sections - 1 else (s, i, j ^ 1)
    )

    weight_grad, _ = together(weight_grad, out)
    weight_grad = weight_product(
        [x_near, x_far],
        [
            (0, ats[1], 0, 0),
            (1, ats[1], 0, 2 * x_count + 1),
            (2, ats[2], 1, 0),
            (3, ats[2], 1, 1),
            (4, ats[3], 0, 2 * x_count),
            (5, ats[3], 0, 1),
        ],
        parts[2:],
        weight_grad,
        final=True,
    )
    passed, weight_grad = together(passed, weight_grad)
    passed, above, below = together(passed, above, below)
    passed = call(
        functools.partial(last_kernel, [2, last, 1]),
        [passed.shape],
        base,
        two,
        above,
        below,
        passed,
        in_specs=[VMEM] * 4 + [HBM],
        out_specs=[HBM],
        scratch_shapes=[pltpu.VMEM((3, rows, width), BF16), pltpu.SemaphoreType.DMA((3,))],
        input_output_aliases={4: 0},
    )[0]
    return passed[None, None], weight_grad[None]


def solution(mesh):
    return jax.shard_map(
        body,
        mesh=mesh,
        in_specs=(
            P("section", "dp", "tensor", None),
            P("section", "dp", "tensor", None),
            P("section", "dp", None, "tensor"),
            P("section", "dp", None, "tensor"),
            P("section", "dp", "tensor"),
        ),
        out_specs=(P("section", "dp", "tensor", None), P("section", "dp", "tensor")),
        check_vma=False,
    )
```

```python
import functools

import jax
import jax.numpy as jnp
from jax import lax
from jax.experimental import pallas as pl
from jax.experimental.pallas import tpu as pltpu
from jax.sharding import PartitionSpec as P

AXES = ("section", "dp", "tensor")
BF16 = jnp.bfloat16
F32 = jnp.float32
VMEM = pl.BlockSpec(memory_space=pltpu.VMEM)
HBM = pl.BlockSpec(memory_space=pltpu.HBM)
NT = (((1,), (1,)), ((), ()))
TN = (((0,), (0,)), ((), ()))
LANES = 128
START = 53


def moved(value, sizes, target):
    sections, replicas, shards = sizes
    pairs = []
    for s in range(sections):
        for r in range(replicas):
            for t in range(shards):
                to_s, to_r, to_t = target(s, r, t)
                pairs.append(
                    ((s * replicas + r) * shards + t, (to_s * replicas + to_r) * shards + to_t)
                )
    return lax.ppermute(value, AXES, pairs)


def together(*values):
    return lax.optimization_barrier(values)


def shifted(r, k, replicas):
    if replicas != 4:
        return lax.rem(r + k % replicas, replicas) if isinstance(r, jax.Array) else (r + k) % replicas
    place = ((r ^ (r >> 1)) + k % 4) & 3
    return place ^ (place >> 1)


def call(kernel, outputs, *arrays, limit=8, flops=0, **more):
    size = sum(v.size * v.dtype.itemsize for v in arrays)
    if flops:
        more["cost_estimate"] = pl.CostEstimate(flops=flops, bytes_accessed=size, transcendentals=0)
    options = dict(in_specs=[VMEM] * len(arrays), out_specs=[VMEM] * len(outputs))
    return pl.pallas_call(
        kernel,
        out_shape=[v if hasattr(v, "dtype") else jax.ShapeDtypeStruct(v, BF16) for v in outputs],
        compiler_params=pltpu.CompilerParams(vmem_limit_bytes=limit * 2**20),
        **{**options, **more},
    )(*arrays)


def added(a, b):
    return (a.astype(F32) + b.astype(F32)).astype(BF16)


def start_kernel(shards, items, grad, gate, x, *refs):
    *outs, grad_here, gate_here, x_here, arrived, x_arrived = refs
    tokens, hidden = grad.shape
    replicas = len(x_here)
    width = x.shape[1] // replicas
    half = outs[0].shape[1]
    copies = []
    for shard in range(shards):
        here = pl.ds(2 * shard * half, 2 * half)
        for i, (source, to) in enumerate(((grad, grad_here), (gate, gate_here))):
            copies.append(pltpu.make_async_copy(source.at[here], to.at[here], arrived.at[i, shard]))
            copies[-1].start()
    x_copies = []
    for device in range(replicas):
        block = shifted(lax.axis_index("dp"), device, replicas)
        columns = pl.ds(pl.multiple_of(block * width, width), width)
        x_copies.append(pltpu.make_async_copy(x.at[:, columns], x_here[device], x_arrived.at[device]))
        x_copies[-1].start()
    for shard in range(shards):
        copies[2 * shard].wait()
        copies[2 * shard + 1].wait()
        for out, (_, cut) in zip(outs, items):
            if cut is None:
                continue
            at = out.shape[0] - hidden // LANES * shards + shard
            here = pl.ds((2 * shard + cut) * half, half)
            for column in range(hidden // LANES):
                lanes = pl.ds(column * LANES, LANES)
                g = gate_here[here, lanes].astype(F32)
                value = grad_here[here, lanes].astype(F32) * g * (0.5 + 0.5 * jnp.tanh(0.5 * g))
                out[at + column * shards] = value.astype(BF16)
    for copy in x_copies:
        copy.wait()
    for out, (of, _) in zip(outs, items):
        at = 0
        for device, cuts in of:
            for column in range(width // LANES):
                for c in cuts:
                    out[at] = x_here[device][c * half : (c + 1) * half, column * LANES : (column + 1) * LANES]
                    at += 1


def held_kernel(source, out, done):
    copy = pltpu.make_async_copy(source, out, done)
    copy.start()
    copy.wait()


def stack_kernel(places, *refs):
    *sources, out = refs
    for source, first, count, to, step in places:
        for i in range(count):
            out[to + i * step] = sources[source][first + i]


def product_kernel(shards, offsets, *refs):
    pieces, w, outs = refs[: len(offsets)], refs[len(offsets)], refs[len(offsets) + 1 :]
    columns = w.shape[1] // LANES
    bit = lax.rem(lax.axis_index("tensor"), 2)
    left = [
        jnp.concatenate([piece[at + c * shards + 2 * m + start] for c in range(columns)], axis=1)
        for start in (bit, 1 - bit)
        for piece, at in zip(pieces, offsets)
        for m in range(shards // 2)
    ]
    out = lax.dot_general(jnp.concatenate(left), w[...], NT, preferred_element_type=F32).astype(BF16)
    rows = out.shape[0] // 2
    for i, (mine, theirs) in enumerate(zip(outs[::2], outs[1::2])):
        n = rows // (len(outs) // 2)
        mine[...] = out[i * n : (i + 1) * n].reshape(mine.shape)
        theirs[...] = out[rows + i * n : rows + (i + 1) * n].reshape(theirs.shape)


def dealt_kernel(shards, offsets, rider, riders, *refs):
    pieces, w, outs = refs[: len(offsets)], refs[len(offsets)], refs[len(offsets) + 1 :]
    columns = w.shape[1] // LANES
    left = [
        jnp.concatenate([piece[at + c * shards + (lax.axis_index("tensor") ^ j)] for c in range(columns)], axis=1)
        for j in range(shards)
        for piece, at in zip(pieces, offsets)
    ]
    total = lax.dot_general(jnp.concatenate(left), w[...], NT, preferred_element_type=F32).astype(BF16)
    rows = total.shape[0] // shards
    for j, out in enumerate(outs):
        if j != rider:
            out[...] = total[j * rows : (j + 1) * rows]
            continue
        half = out.shape[1]
        for n in range(rows // half):
            for c in range(total.shape[1] // LANES):
                out[c * (rows // half) + n] = total[
                    j * rows + n * half : j * rows + (n + 1) * half, c * LANES : (c + 1) * LANES
                ]
        for piece, first, count, to, step in riders:
            for i in range(count):
                out[rows // half * (total.shape[1] // LANES) + to + i * step] = pieces[piece][first + i]


def total_kernel(count, rider, *refs):
    parts, outs = refs[:count], refs[count:]
    rows, width = parts[0].shape
    total = sum(part[...].astype(F32) for j, part in enumerate(parts) if j != rider)
    at = 0
    for out in outs:
        value = total[at : at + out.shape[0]]
        if rider is not None:
            packed = parts[rider]
            half = packed.shape[1]
            blocks = [
                jnp.concatenate(
                    [packed[c * (rows // half) + n] for c in range(width // LANES)], axis=1
                )
                for n in range(at // half, (at + out.shape[0]) // half)
            ]
            value = value + jnp.concatenate(blocks).astype(F32)
        out[...] = value.astype(BF16)
        at += out.shape[0]


def fold_kernel(step, *refs):
    *pairs, keep, give = refs
    bit = lax.rem(lax.div(lax.axis_index("tensor"), step), 2)
    at = 0
    for mine, got in zip(pairs[::2], pairs[1::2]):
        n, shards = mine.shape[:2]
        for i in range(n):
            for m in range(shards // 2):
                for to, start in ((keep, bit), (give, 1 - bit)):
                    to[at + i, m] = added(mine[i, 2 * m + start], got[i, 2 * m + start])
        at += n


def sum_kernel(mine, got, *outs):
    at = 0
    for out in outs:
        n = out.shape[0] // mine.shape[2]
        here = pl.ds(at, n)
        out[...] = added(mine[here], got[here]).reshape(out.shape)
        at += n


def crossed_kernel(mine, got, first, second, above, below):
    half = first.shape[0]
    total = added(mine[...], got[...]).reshape(-1, first.shape[1])
    above[:half], above[half:] = total[:half], second[...]
    below[:half], below[half:] = first[...], total[half:]


def weight_kernel(groups, pairs, scale, count, *refs):
    inputs, rest = refs[:count], refs[count:]
    *rest, out, right = rest
    many = 1 + max(p[0] for p in pairs)
    parts, so_far = rest[:many], rest[many:]
    half = parts[0].shape[1]
    hidden = out.shape[1]
    shards = len(groups[0])

    @pl.when(pl.program_id(0) == 0)
    def _():
        row = 0
        for part, at, _, _ in pairs:
            for j in range(shards):
                shard = lax.axis_index("tensor") ^ j
                for c in range(hidden // LANES):
                    right[pl.ds(row, half), pl.ds(c * LANES, LANES)] = parts[part][at + c * shards + shard]
                row += half

    tile = out.shape[0]
    first = pl.program_id(0) * (tile // LANES)
    left = []
    for _, _, group, at in pairs:
        for j in range(shards):
            block, start = groups[group][j]
            columns = [inputs[block][start + at + 2 * (first + c)] for c in range(tile // LANES)]
            left.append(jnp.concatenate(columns, axis=1))
    total = lax.dot_general(jnp.concatenate(left), right[...], TN, preferred_element_type=F32)
    for already in so_far:
        total += already[pl.ds(pl.multiple_of(pl.program_id(0) * tile, tile), tile)]
    out[...] = (total / scale).astype(out.dtype)


def passed_kernel(base, piece, out):
    width = piece.shape[1]
    sent = lax.axis_index("section") < lax.axis_size("section") - 1
    out[...] = jnp.where(sent, base[...], jnp.zeros(base.shape, BF16))
    here = (slice(None), pl.ds(pl.multiple_of(lax.axis_index("dp") * width, width), width))
    out[here] = jnp.where(sent, added(base[here], piece[...]), jnp.zeros(piece.shape, BF16))


def last_kernel(blocks, base, *refs):
    *pieces, _, out, total, done = refs
    width = pieces[0].shape[1]
    replicas = base.shape[1] // width
    sent = lax.axis_index("section") < lax.axis_size("section") - 1
    copies = []
    for i, (block, piece) in enumerate(zip(blocks, pieces)):
        device = shifted(lax.axis_index("dp"), block, replicas)
        columns = pl.ds(pl.multiple_of(device * width, width), width)
        total[i] = jnp.where(sent, added(base[:, columns], piece[...]), jnp.zeros(piece.shape, BF16))
        copies.append(pltpu.make_async_copy(total.at[i], out.at[:, columns], done.at[i]))
        copies[-1].start()
    for copy in copies:
        copy.wait()


def body(section_input, carried_grad, hidden_grad, saved_gate, w_up):
    sizes = tuple(lax.axis_size(a) for a in AXES)
    sections, replicas, shards = sizes
    grad, gate, x = hidden_grad[0, 0], saved_gate[0, 0], section_input[0, 0]
    w = w_up[0]
    width, hidden = w.shape
    tokens, rows = grad.shape[0], x.shape[0]
    half = rows // 2
    last, middle = replicas - 1, replicas // 2
    up_count, x_count = hidden // LANES * shards, width // LANES

    def up(value):
        return moved(value, sizes, lambda s, i, j: (s, shifted(i, 1, replicas), j))

    def down(value):
        return moved(value, sizes, lambda s, i, j: (s, shifted(i, -1, replicas), j))

    def returned(value, k):
        return moved(
            value,
            sizes,
            lambda s, i, j: (s - 1, shifted(i, -k, replicas), j) if s else (sections - 1, i, j),
        )

    def across(value, step):
        return moved(value, sizes, lambda s, i, j: (s, i, j ^ step))

    def product(*pieces, groups=1, flops=0):
        share = (len(pieces) // groups, shards // 2, half, width)
        kernel = functools.partial(product_kernel, shards, [at for _, at in pieces])
        return call(kernel, [share] * (2 * groups), *[piece for piece, _ in pieces], w, flops=flops)

    def summed(pieces, halves, rider=None, riders=()):
        kernel = functools.partial(dealt_kernel, shards, [at for _, at in pieces], rider, riders)
        shares = [(len(pieces) * half, width)] * shards
        own = len(pieces) * x_count
        if rider is not None:
            shares[rider] = (own + sum(count for _, _, count, _, _ in riders), half, LANES)
        mine, *others = call(kernel, shares, *[piece for piece, _ in pieces], w)
        others = [across(v, j + 1) for j, v in enumerate(others)]
        kernel = functools.partial(total_kernel, shards, rider)
        outs = call(kernel, [(n * half, width) for n in halves], mine, *others)
        return outs, others[rider - 1] if rider is not None else None

    def fold(step, *pairs):
        n, m = sum(v.shape[0] for v in pairs[::2]), pairs[0].shape[1]
        share = (n, m // 2, half, width)
        return call(functools.partial(fold_kernel, step), [share, share], *pairs)

    def finished(mine, got, *halves):
        step = 4
        while step < shards:
            mine, give = fold(step, mine, got)
            got = across(give, step)
            step *= 2
        return call(sum_kernel, [(n * half, width) for n in halves], mine, got)

    def stacked(count, places, *sources):
        return call(functools.partial(stack_kernel, places), [(count, half, LANES)], *sources)[0]

    def doubled(block, step, steps):
        for _ in range(steps):
            n = block.shape[0]
            places = [(i, 0, n, i * n, 1) for i in range(2)]
            block = stacked(2 * n, places, block, across(block, step))
            step //= 2
        return block

    far_step, steps = shards // 2, shards.bit_length() - 1
    order = [0]
    for i in range(steps - 1):
        order += [j + (far_step >> i) for j in order]

    tile = 256

    def weight_product(xs, pairs, parts, *so_far, final):
        groups, at = [], 0
        for x in xs:
            group = [None] * shards
            for i, j in enumerate(order):
                for other in (0, 1):
                    if len(x) == 2:
                        group[j ^ other] = (at + other, i * (x[0].shape[0] // len(order)))
                    else:
                        group[j ^ other] = (at + (j ^ other), 0)
            groups.append(group)
            at += len(x)
        kernel = functools.partial(weight_kernel, groups, pairs, replicas if final else 1, at)
        return call(
            kernel,
            [jax.ShapeDtypeStruct((width, hidden), BF16 if final else F32)],
            *[v for x in xs for v in x],
            *parts,
            *so_far,
            grid=(width // tile,),
            out_specs=[pl.BlockSpec((tile, hidden), lambda i: (i, 0))],
            scratch_shapes=[pltpu.VMEM((len(pairs) * shards * half, hidden), BF16)],
            limit=20,
        )[0]

    both = (0, 1)
    items = [[(d, both) for d in range(1, (replicas + 1) // 2)], [(last + 1 - d, both) for d in range(1, (replicas + 1) // 2)]]
    if replicas % 2 == 0:
        for cut in both:
            items[cut].append((middle, (cut,)))
    items = [(items[0], 0), (items[1], 1), ([(0, both)], None)]
    counts = [sum(x_count * len(cuts) for _, cuts in of) + (cut is not None) * up_count for of, cut in items]
    a, b, x_own = call(
        functools.partial(start_kernel, shards, items),
        [(n, half, LANES) for n in counts],
        grad,
        gate,
        x,
        in_specs=[HBM] * 3,
        scratch_shapes=[pltpu.VMEM((tokens, hidden), BF16)] * 2
        + [[pltpu.VMEM((rows, width), BF16)] * replicas]
        + [pltpu.SemaphoreType.DMA((2, shards)), pltpu.SemaphoreType.DMA((replicas,))],
        limit=START,
    )
    a_next, b_next = up(a), down(b)
    carried, *_ = together(carried_grad[0, 0], a, b)
    base = returned(carried, 0)
    w = call(held_kernel, [w.shape], w, in_specs=[HBM], scratch_shapes=[pltpu.SemaphoreType.DMA])[0]
    at = a.shape[0] - up_count
    a_parts, b_parts, ats = [a], [b], [at]
    (out,), _ = summed([(a, at), (b, at)], [2])
    x_own = doubled(x_own, far_step, steps - 1)
    x_own = [x_own, across(x_own, 1)]

    a, b, base, out, *x_own = together(a_next, b_next, base, out, *x_own)
    a_parts.append(a)
    b_parts.append(b)
    ats.append(at)
    a_next, b_next = up(a[2 * x_count :]), down(b[2 * x_count :])
    zero = returned(out, 0)
    keep_a, give_a, keep_b, give_b = product((a, at), (b, at), groups=2)
    keep, give = fold(2, keep_a, across(give_a, 1), keep_b, across(give_b, 1))
    nears = finished(keep, across(give, 2), 1, 1)
    x_near = stacked(4 * x_count, [(i, 0, 2 * x_count, 2 * i * x_count, 1) for i in range(2)], a, b)
    x_near, step = {0: x_near}, far_step
    while step > 1:
        x_near |= {j + step: across(v, step) for j, v in x_near.items()}
        step //= 2
    blocks = sorted(x_near)
    x_near = [x_near[j] for j in blocks]

    at -= 2 * x_count
    weight_grad = weight_product(
        [x_own], [(0, ats[0], 0, 0), (1, ats[0], 0, 1)], [a_parts[0], b_parts[0]], final=False
    )
    a, b, zero, weight_grad, *nears = together(a_next, b_next, zero, weight_grad, *nears)
    a_parts.append(a)
    b_parts.append(b)
    ats.append(at)
    a_next, b_next = up(a[x_count:]), down(b[x_count:])
    far_a, far_b, *x_near = together(a, b, *x_near)
    riders = [(i, 0, x_count, i, 2) for i in range(2)]
    (out,), x_far = summed([(far_a, at), (far_b, at)], [2], far_step, riders)

    at -= x_count
    a, b = a_next, b_next
    a_parts.append(a)
    b_parts.append(b)
    ats.append(at)
    keep, give = product((a, at), (b, at), flops=2 * tokens * hidden * width)
    passed = call(passed_kernel, [(rows, replicas * width)], base, zero)[0]
    x_far, give, out, passed = together(x_far, give, out, passed)
    keep, give = fold(2, keep, across(give, 1))
    got = across(give, 2)
    out, _ = together(out, give)
    two = returned(out, 0)
    x_near = [v for pair in ((v, across(v, 1)) for v in x_near) for v in pair]
    places = [(i, 0, x_count, i, 2) for i in range(2)] + [(2, 2 * x_count, 2 * x_count, 2 * x_count, 1)]
    x_far = stacked(4 * x_count, places, a_parts[2], b_parts[2], x_far)
    x_far = doubled(x_far, far_step // 2, steps - 2)
    x_far = [x_far, across(x_far, 1)]

    parts = [v for pair_of in zip(a_parts, b_parts) for v in pair_of]
    step = 4
    while step < shards:
        keep, give = fold(step, keep, got)
        got = across(give, step)
        step *= 2
    above, below = call(crossed_kernel, [(rows, width)] * 2, keep, got, *nears)
    out = above
    above, below = returned(above, -1), returned(below, 1)
    two = moved(
        two, sizes, lambda s, i, j: (s, shifted(i, -2, replicas), j) if s < sections - 1 else (s, i, j ^ 1)
    )

    weight_grad, _ = together(weight_grad, out)
    weight_grad = weight_product(
        [x_near, x_far],
        [
            (0, ats[1], 0, 0),
            (1, ats[1], 0, 2 * x_count + 1),
            (2, ats[2], 1, 0),
            (3, ats[2], 1, 1),
            (4, ats[3], 0, 2 * x_count),
            (5, ats[3], 0, 1),
        ],
        parts[2:],
        weight_grad,
        final=True,
    )
    passed, weight_grad = together(passed, weight_grad)
    passed, above, below = together(passed, above, below)
    passed = call(
        functools.partial(last_kernel, [2, last, 1]),
        [passed.shape],
        base,
        two,
        above,
        below,
        passed,
        in_specs=[VMEM] * 4 + [HBM],
        out_specs=[HBM],
        scratch_shapes=[pltpu.VMEM((3, rows, width), BF16), pltpu.SemaphoreType.DMA((3,))],
        input_output_aliases={4: 0},
    )[0]
    return passed[None, None], weight_grad[None]


def solution(mesh):
    return jax.shard_map(
        body,
        mesh=mesh,
        in_specs=(
            P("section", "dp", "tensor", None),
            P("section", "dp", "tensor", None),
            P("section", "dp", None, "tensor"),
            P("section", "dp", None, "tensor"),
            P("section", "dp", "tensor"),
        ),
        out_specs=(P("section", "dp", "tensor", None), P("section", "dp", "tensor")),
        check_vma=False,
    )
```

```python
import functools

import jax
import jax.numpy as jnp
from jax import lax
from jax.experimental import pallas as pl
from jax.experimental.pallas import tpu as pltpu
from jax.sharding import PartitionSpec as P

AXES = ("section", "dp", "tensor")
BF16 = jnp.bfloat16
F32 = jnp.float32
VMEM = pl.BlockSpec(memory_space=pltpu.VMEM)
HBM = pl.BlockSpec(memory_space=pltpu.HBM)
NT = (((1,), (1,)), ((), ()))
TN = (((0,), (0,)), ((), ()))
LANES = 128
START = 53


def moved(value, sizes, target):
    sections, replicas, shards = sizes
    pairs = []
    for s in range(sections):
        for r in range(replicas):
            for t in range(shards):
                to_s, to_r, to_t = target(s, r, t)
                pairs.append(
                    ((s * replicas + r) * shards + t, (to_s * replicas + to_r) * shards + to_t)
                )
    return lax.ppermute(value, AXES, pairs)


def together(*values):
    return lax.optimization_barrier(values)


def shifted(r, k, replicas):
    if replicas != 4:
        return lax.rem(r + k % replicas, replicas) if isinstance(r, jax.Array) else (r + k) % replicas
    place = ((r ^ (r >> 1)) + k % 4) & 3
    return place ^ (place >> 1)


def call(kernel, outputs, *arrays, limit=8, flops=0, **more):
    size = sum(v.size * v.dtype.itemsize for v in arrays)
    if flops:
        more["cost_estimate"] = pl.CostEstimate(flops=flops, bytes_accessed=size, transcendentals=0)
    options = dict(in_specs=[VMEM] * len(arrays), out_specs=[VMEM] * len(outputs))
    return pl.pallas_call(
        kernel,
        out_shape=[v if hasattr(v, "dtype") else jax.ShapeDtypeStruct(v, BF16) for v in outputs],
        compiler_params=pltpu.CompilerParams(vmem_limit_bytes=limit * 2**20),
        **{**options, **more},
    )(*arrays)


def added(a, b):
    return (a.astype(F32) + b.astype(F32)).astype(BF16)


def start_kernel(shards, items, grad, gate, x, *refs):
    *outs, grad_here, gate_here, x_here, arrived, x_arrived = refs
    tokens, hidden = grad.shape
    replicas = len(x_here)
    width = x.shape[1] // replicas
    half = outs[0].shape[1]
    copies = []
    for shard in range(shards):
        here = pl.ds(2 * shard * half, 2 * half)
        for i, (source, to) in enumerate(((grad, grad_here), (gate, gate_here))):
            copies.append(pltpu.make_async_copy(source.at[here], to.at[here], arrived.at[i, shard]))
            copies[-1].start()
    x_copies = []
    for device in range(replicas):
        block = shifted(lax.axis_index("dp"), device, replicas)
        columns = pl.ds(pl.multiple_of(block * width, width), width)
        x_copies.append(pltpu.make_async_copy(x.at[:, columns], x_here[device], x_arrived.at[device]))
        x_copies[-1].start()
    for shard in range(shards):
        copies[2 * shard].wait()
        copies[2 * shard + 1].wait()
        for out, (_, cut) in zip(outs, items):
            if cut is None:
                continue
            at = out.shape[0] - hidden // LANES * shards + shard
            here = pl.ds((2 * shard + cut) * half, half)
            for column in range(hidden // LANES):
                lanes = pl.ds(column * LANES, LANES)
                g = gate_here[here, lanes].astype(F32)
                value = grad_here[here, lanes].astype(F32) * g * (0.5 + 0.5 * jnp.tanh(0.5 * g))
                out[at + column * shards] = value.astype(BF16)
    for copy in x_copies:
        copy.wait()
    for out, (of, _) in zip(outs, items):
        at = 0
        for device, cuts in of:
            for column in range(width // LANES):
                for c in cuts:
                    out[at] = x_here[device][c * half : (c + 1) * half, column * LANES : (column + 1) * LANES]
                    at += 1


def held_kernel(source, out, done):
    copy = pltpu.make_async_copy(source, out, done)
    copy.start()
    copy.wait()


def stack_kernel(places, *refs):
    *sources, out = refs
    for source, first, count, to, step in places:
        for i in range(count):
            out[to + i * step] = sources[source][first + i]


def product_kernel(shards, offsets, *refs):
    pieces, w, outs = refs[: len(offsets)], refs[len(offsets)], refs[len(offsets) + 1 :]
    columns = w.shape[1] // LANES
    bit = lax.rem(lax.axis_index("tensor"), 2)
    left = [
        jnp.concatenate([piece[at + c * shards + 2 * m + start] for c in range(columns)], axis=1)
        for start in (bit, 1 - bit)
        for piece, at in zip(pieces, offsets)
        for m in range(shards // 2)
    ]
    out = lax.dot_general(jnp.concatenate(left), w[...], NT, preferred_element_type=F32).astype(BF16)
    rows = out.shape[0] // 2
    for i, (mine, theirs) in enumerate(zip(outs[::2], outs[1::2])):
        n = rows // (len(outs) // 2)
        mine[...] = out[i * n : (i + 1) * n].reshape(mine.shape)
        theirs[...] = out[rows + i * n : rows + (i + 1) * n].reshape(theirs.shape)


def dealt_kernel(shards, offsets, rider, riders, *refs):
    pieces, w, outs = refs[: len(offsets)], refs[len(offsets)], refs[len(offsets) + 1 :]
    columns = w.shape[1] // LANES
    left = [
        jnp.concatenate([piece[at + c * shards + (lax.axis_index("tensor") ^ j)] for c in range(columns)], axis=1)
        for j in range(shards)
        for piece, at in zip(pieces, offsets)
    ]
    total = lax.dot_general(jnp.concatenate(left), w[...], NT, preferred_element_type=F32).astype(BF16)
    rows = total.shape[0] // shards
    for j, out in enumerate(outs):
        if j != rider:
            out[...] = total[j * rows : (j + 1) * rows]
            continue
        half = out.shape[1]
        for n in range(rows // half):
            for c in range(total.shape[1] // LANES):
                out[c * (rows // half) + n] = total[
                    j * rows + n * half : j * rows + (n + 1) * half, c * LANES : (c + 1) * LANES
                ]
        for piece, first, count, to, step in riders:
            for i in range(count):
                out[rows // half * (total.shape[1] // LANES) + to + i * step] = pieces[piece][first + i]


def total_kernel(count, rider, *refs):
    parts, outs = refs[:count], refs[count:]
    rows, width = parts[0].shape
    total = sum(part[...].astype(F32) for j, part in enumerate(parts) if j != rider)
    at = 0
    for out in outs:
        value = total[at : at + out.shape[0]]
        if rider is not None:
            packed = parts[rider]
            half = packed.shape[1]
            blocks = [
                jnp.concatenate(
                    [packed[c * (rows // half) + n] for c in range(width // LANES)], axis=1
                )
                for n in range(at // half, (at + out.shape[0]) // half)
            ]
            value = value + jnp.concatenate(blocks).astype(F32)
        out[...] = value.astype(BF16)
        at += out.shape[0]


def fold_kernel(step, *refs):
    *pairs, keep, give = refs
    bit = lax.rem(lax.div(lax.axis_index("tensor"), step), 2)
    at = 0
    for mine, got in zip(pairs[::2], pairs[1::2]):
        n, shards = mine.shape[:2]
        for i in range(n):
            for m in range(shards // 2):
                for to, start in ((keep, bit), (give, 1 - bit)):
                    to[at + i, m] = added(mine[i, 2 * m + start], got[i, 2 * m + start])
        at += n


def sum_kernel(mine, got, *outs):
    at = 0
    for out in outs:
        n = out.shape[0] // mine.shape[2]
        here = pl.ds(at, n)
        out[...] = added(mine[here], got[here]).reshape(out.shape)
        at += n


def crossed_kernel(mine, got, first, second, above, below):
    half = first.shape[0]
    total = added(mine[...], got[...]).reshape(-1, first.shape[1])
    above[:half], above[half:] = total[:half], second[...]
    below[:half], below[half:] = first[...], total[half:]


def weight_kernel(groups, pairs, scale, count, *refs):
    inputs, rest = refs[:count], refs[count:]
    *rest, out, right = rest
    many = 1 + max(p[0] for p in pairs)
    parts, so_far = rest[:many], rest[many:]
    half = parts[0].shape[1]
    hidden = out.shape[1]
    shards = len(groups[0])

    @pl.when(pl.program_id(0) == 0)
    def _():
        row = 0
        for part, at, _, _ in pairs:
            for j in range(shards):
                shard = lax.axis_index("tensor") ^ j
                for c in range(hidden // LANES):
                    right[pl.ds(row, half), pl.ds(c * LANES, LANES)] = parts[part][at + c * shards + shard]
                row += half

    tile = out.shape[0]
    first = pl.program_id(0) * (tile // LANES)
    left = []
    for _, _, group, at in pairs:
        for j in range(shards):
            block, start = groups[group][j]
            columns = [inputs[block][start + at + 2 * (first + c)] for c in range(tile // LANES)]
            left.append(jnp.concatenate(columns, axis=1))
    total = lax.dot_general(jnp.concatenate(left), right[...], TN, preferred_element_type=F32)
    for already in so_far:
        total += already[pl.ds(pl.multiple_of(pl.program_id(0) * tile, tile), tile)]
    out[...] = (total / scale).astype(out.dtype)


def apart_kernel(carried, out, done):
    _, _, width = out.shape
    copies = []
    for i in range(out.shape[0]):
        device = shifted(lax.axis_index("dp"), i + 1, out.shape[0] + 1)
        columns = pl.ds(pl.multiple_of(device * width, width), width)
        copies.append(pltpu.make_async_copy(carried.at[:, columns], out.at[i], done.at[i]))
        copies[-1].start()
    for copy in copies:
        copy.wait()


def merged_kernel(carried, piece, out):
    width = piece.shape[1]
    columns = pl.ds(pl.multiple_of(lax.axis_index("dp") * width, width), width)
    out[...] = added(carried[:, columns], piece[...])


def first_kernel(piece, out, total, done):
    width = piece.shape[1]
    columns = pl.ds(pl.multiple_of(lax.axis_index("dp") * width, width), width)
    sent = lax.axis_index("section") < lax.axis_size("section") - 1
    total[...] = jnp.where(sent, piece[...], jnp.zeros(piece.shape, BF16))
    copy = pltpu.make_async_copy(total, out.at[:, columns], done)
    copy.start()
    copy.wait()


def last_kernel(blocks, base, *refs):
    *pieces, _, out, total, done = refs
    width = pieces[0].shape[1]
    replicas = base.shape[0] + 1
    sent = lax.axis_index("section") < lax.axis_size("section") - 1
    copies = []
    for i, (block, piece) in enumerate(zip(blocks, pieces)):
        device = shifted(lax.axis_index("dp"), block, replicas)
        columns = pl.ds(pl.multiple_of(device * width, width), width)
        total[i] = jnp.where(sent, added(base[block - 1], piece[...]), jnp.zeros(piece.shape, BF16))
        copies.append(pltpu.make_async_copy(total.at[i], out.at[:, columns], done.at[i]))
        copies[-1].start()
    for copy in copies:
        copy.wait()


def body(section_input, carried_grad, hidden_grad, saved_gate, w_up):
    sizes = tuple(lax.axis_size(a) for a in AXES)
    sections, replicas, shards = sizes
    grad, gate, x = hidden_grad[0, 0], saved_gate[0, 0], section_input[0, 0]
    w = w_up[0]
    width, hidden = w.shape
    tokens, rows = grad.shape[0], x.shape[0]
    half = rows // 2
    last, middle = replicas - 1, replicas // 2
    up_count, x_count = hidden // LANES * shards, width // LANES

    def up(value):
        return moved(value, sizes, lambda s, i, j: (s, shifted(i, 1, replicas), j))

    def down(value):
        return moved(value, sizes, lambda s, i, j: (s, shifted(i, -1, replicas), j))

    def returned(value, k):
        return moved(
            value,
            sizes,
            lambda s, i, j: (s - 1, shifted(i, -k, replicas), j) if s else (sections - 1, i, j),
        )

    def across(value, step):
        return moved(value, sizes, lambda s, i, j: (s, i, j ^ step))

    def product(*pieces, groups=1, flops=0):
        share = (len(pieces) // groups, shards // 2, half, width)
        kernel = functools.partial(product_kernel, shards, [at for _, at in pieces])
        return call(kernel, [share] * (2 * groups), *[piece for piece, _ in pieces], w, flops=flops)

    def summed(pieces, halves, rider=None, riders=()):
        kernel = functools.partial(dealt_kernel, shards, [at for _, at in pieces], rider, riders)
        shares = [(len(pieces) * half, width)] * shards
        own = len(pieces) * x_count
        if rider is not None:
            shares[rider] = (own + sum(count for _, _, count, _, _ in riders), half, LANES)
        mine, *others = call(kernel, shares, *[piece for piece, _ in pieces], w)
        others = [across(v, j + 1) for j, v in enumerate(others)]
        kernel = functools.partial(total_kernel, shards, rider)
        outs = call(kernel, [(n * half, width) for n in halves], mine, *others)
        return outs, others[rider - 1] if rider is not None else None

    def fold(step, *pairs):
        n, m = sum(v.shape[0] for v in pairs[::2]), pairs[0].shape[1]
        share = (n, m // 2, half, width)
        return call(functools.partial(fold_kernel, step), [share, share], *pairs)

    def finished(mine, got, *halves):
        step = 4
        while step < shards:
            mine, give = fold(step, mine, got)
            got = across(give, step)
            step *= 2
        return call(sum_kernel, [(n * half, width) for n in halves], mine, got)

    def stacked(count, places, *sources):
        return call(functools.partial(stack_kernel, places), [(count, half, LANES)], *sources)[0]

    def doubled(block, step, steps):
        for _ in range(steps):
            n = block.shape[0]
            places = [(i, 0, n, i * n, 1) for i in range(2)]
            block = stacked(2 * n, places, block, across(block, step))
            step //= 2
        return block

    far_step, steps = shards // 2, shards.bit_length() - 1
    order = [0]
    for i in range(steps - 1):
        order += [j + (far_step >> i) for j in order]

    tile = 256

    def weight_product(xs, pairs, parts, *so_far, final):
        groups, at = [], 0
        for x in xs:
            group = [None] * shards
            for i, j in enumerate(order):
                for other in (0, 1):
                    if len(x) == 2:
                        group[j ^ other] = (at + other, i * (x[0].shape[0] // len(order)))
                    else:
                        group[j ^ other] = (at + (j ^ other), 0)
            groups.append(group)
            at += len(x)
        kernel = functools.partial(weight_kernel, groups, pairs, replicas if final else 1, at)
        return call(
            kernel,
            [jax.ShapeDtypeStruct((width, hidden), BF16 if final else F32)],
            *[v for x in xs for v in x],
            *parts,
            *so_far,
            grid=(width // tile,),
            out_specs=[pl.BlockSpec((tile, hidden), lambda i: (i, 0))],
            scratch_shapes=[pltpu.VMEM((len(pairs) * shards * half, hidden), BF16)],
            limit=20,
        )[0]

    both = (0, 1)
    items = [[(d, both) for d in range(1, (replicas + 1) // 2)], [(last + 1 - d, both) for d in range(1, (replicas + 1) // 2)]]
    if replicas % 2 == 0:
        for cut in both:
            items[cut].append((middle, (cut,)))
    items = [(items[0], 0), (items[1], 1), ([(0, both)], None)]
    counts = [sum(x_count * len(cuts) for _, cuts in of) + (cut is not None) * up_count for of, cut in items]
    a, b, x_own = call(
        functools.partial(start_kernel, shards, items),
        [(n, half, LANES) for n in counts],
        grad,
        gate,
        x,
        in_specs=[HBM] * 3,
        scratch_shapes=[pltpu.VMEM((tokens, hidden), BF16)] * 2
        + [[pltpu.VMEM((rows, width), BF16)] * replicas]
        + [pltpu.SemaphoreType.DMA((2, shards)), pltpu.SemaphoreType.DMA((replicas,))],
        limit=START,
    )
    a_next, b_next = up(a), down(b)
    carried, *_ = together(carried_grad[0, 0], a, b)
    base = call(
        apart_kernel,
        [(last, rows, width)],
        carried,
        in_specs=[HBM],
        scratch_shapes=[pltpu.SemaphoreType.DMA((last,))],
    )[0]
    base = returned(base, 0)
    w = call(held_kernel, [w.shape], w, in_specs=[HBM], scratch_shapes=[pltpu.SemaphoreType.DMA])[0]
    at = a.shape[0] - up_count
    a_parts, b_parts, ats = [a], [b], [at]
    (out,), _ = summed([(a, at), (b, at)], [2])
    x_own = doubled(x_own, far_step, steps - 1)
    x_own = [x_own, across(x_own, 1)]

    a, b, base, out, *x_own = together(a_next, b_next, base, out, *x_own)
    a_parts.append(a)
    b_parts.append(b)
    ats.append(at)
    a_next, b_next = up(a[2 * x_count :]), down(b[2 * x_count :])
    zero = returned(call(merged_kernel, [(rows, width)], carried_grad[0, 0], out)[0], 0)
    keep_a, give_a, keep_b, give_b = product((a, at), (b, at), groups=2)
    keep, give = fold(2, keep_a, across(give_a, 1), keep_b, across(give_b, 1))
    nears = finished(keep, across(give, 2), 1, 1)
    x_near = stacked(4 * x_count, [(i, 0, 2 * x_count, 2 * i * x_count, 1) for i in range(2)], a, b)
    x_near, step = {0: x_near}, far_step
    while step > 1:
        x_near |= {j + step: across(v, step) for j, v in x_near.items()}
        step //= 2
    blocks = sorted(x_near)
    x_near = [x_near[j] for j in blocks]

    at -= 2 * x_count
    weight_grad = weight_product(
        [x_own], [(0, ats[0], 0, 0), (1, ats[0], 0, 1)], [a_parts[0], b_parts[0]], final=False
    )
    a, b, zero, weight_grad, *nears = together(a_next, b_next, zero, weight_grad, *nears)
    a_parts.append(a)
    b_parts.append(b)
    ats.append(at)
    a_next, b_next = up(a[x_count:]), down(b[x_count:])
    far_a, far_b, *x_near = together(a, b, *x_near)
    riders = [(i, 0, x_count, i, 2) for i in range(2)]
    (out,), x_far = summed([(far_a, at), (far_b, at)], [2], far_step, riders)

    at -= x_count
    a, b = a_next, b_next
    a_parts.append(a)
    b_parts.append(b)
    ats.append(at)
    keep, give = product((a, at), (b, at), flops=2 * tokens * hidden * width)
    passed = call(
        first_kernel,
        [(rows, replicas * width)],
        zero,
        out_specs=[HBM],
        scratch_shapes=[pltpu.VMEM((rows, width), BF16), pltpu.SemaphoreType.DMA],
    )[0]
    x_far, give, out, passed = together(x_far, give, out, passed)
    keep, give = fold(2, keep, across(give, 1))
    got = across(give, 2)
    out, _ = together(out, give)
    two = returned(out, 0)
    x_near = [v for pair in ((v, across(v, 1)) for v in x_near) for v in pair]
    places = [(i, 0, x_count, i, 2) for i in range(2)] + [(2, 2 * x_count, 2 * x_count, 2 * x_count, 1)]
    x_far = stacked(4 * x_count, places, a_parts[2], b_parts[2], x_far)
    x_far = doubled(x_far, far_step // 2, steps - 2)
    x_far = [x_far, across(x_far, 1)]

    parts = [v for pair_of in zip(a_parts, b_parts) for v in pair_of]
    step = 4
    while step < shards:
        keep, give = fold(step, keep, got)
        got = across(give, step)
        step *= 2
    above, below = call(crossed_kernel, [(rows, width)] * 2, keep, got, *nears)
    out = above
    above, below = returned(above, -1), returned(below, 1)
    two = moved(
        two, sizes, lambda s, i, j: (s, shifted(i, -2, replicas), j) if s < sections - 1 else (s, i, j ^ 1)
    )

    weight_grad, _ = together(weight_grad, out)
    weight_grad = weight_product(
        [x_near, x_far],
        [
            (0, ats[1], 0, 0),
            (1, ats[1], 0, 2 * x_count + 1),
            (2, ats[2], 1, 0),
            (3, ats[2], 1, 1),
            (4, ats[3], 0, 2 * x_count),
            (5, ats[3], 0, 1),
        ],
        parts[2:],
        weight_grad,
        final=True,
    )
    passed, weight_grad = together(passed, weight_grad)
    passed, above, below = together(passed, above, below)
    passed = call(
        functools.partial(last_kernel, [2, last, 1]),
        [passed.shape],
        base,
        two,
        above,
        below,
        passed,
        in_specs=[VMEM] * 4 + [HBM],
        out_specs=[HBM],
        scratch_shapes=[pltpu.VMEM((3, rows, width), BF16), pltpu.SemaphoreType.DMA((3,))],
        input_output_aliases={4: 0},
    )[0]
    return passed[None, None], weight_grad[None]


def solution(mesh):
    return jax.shard_map(
        body,
        mesh=mesh,
        in_specs=(
            P("section", "dp", "tensor", None),
            P("section", "dp", "tensor", None),
            P("section", "dp", None, "tensor"),
            P("section", "dp", None, "tensor"),
            P("section", "dp", "tensor"),
        ),
        out_specs=(P("section", "dp", "tensor", None), P("section", "dp", "tensor")),
        check_vma=False,
    )
```

```python
import functools

import jax
import jax.numpy as jnp
from jax import lax
from jax.experimental import pallas as pl
from jax.experimental.pallas import tpu as pltpu
from jax.sharding import PartitionSpec as P

AXES = ("section", "dp", "tensor")
BF16 = jnp.bfloat16
F32 = jnp.float32
VMEM = pl.BlockSpec(memory_space=pltpu.VMEM)
HBM = pl.BlockSpec(memory_space=pltpu.HBM)
NT = (((1,), (1,)), ((), ()))
TN = (((0,), (0,)), ((), ()))
LANES = 128
START = 53


def moved(value, sizes, target):
    sections, replicas, shards = sizes
    pairs = []
    for s in range(sections):
        for r in range(replicas):
            for t in range(shards):
                to_s, to_r, to_t = target(s, r, t)
                pairs.append(
                    ((s * replicas + r) * shards + t, (to_s * replicas + to_r) * shards + to_t)
                )
    return lax.ppermute(value, AXES, pairs)


def together(*values):
    return lax.optimization_barrier(values)


def shifted(r, k, replicas):
    if replicas != 4:
        return lax.rem(r + k % replicas, replicas) if isinstance(r, jax.Array) else (r + k) % replicas
    place = ((r ^ (r >> 1)) + k % 4) & 3
    return place ^ (place >> 1)


def call(kernel, outputs, *arrays, limit=8, flops=0, **more):
    size = sum(v.size * v.dtype.itemsize for v in arrays)
    if flops:
        more["cost_estimate"] = pl.CostEstimate(flops=flops, bytes_accessed=size, transcendentals=0)
    options = dict(in_specs=[VMEM] * len(arrays), out_specs=[VMEM] * len(outputs))
    return pl.pallas_call(
        kernel,
        out_shape=[v if hasattr(v, "dtype") else jax.ShapeDtypeStruct(v, BF16) for v in outputs],
        compiler_params=pltpu.CompilerParams(vmem_limit_bytes=limit * 2**20),
        **{**options, **more},
    )(*arrays)


def added(a, b):
    return (a.astype(F32) + b.astype(F32)).astype(BF16)


def start_kernel(shards, items, grad, gate, x, *refs):
    *outs, grad_here, gate_here, x_here, arrived, x_arrived = refs
    tokens, hidden = grad.shape
    replicas = len(x_here)
    width = x.shape[1] // replicas
    half = outs[0].shape[1]
    copies = []
    for shard in range(shards):
        here = pl.ds(2 * shard * half, 2 * half)
        for i, (source, to) in enumerate(((grad, grad_here), (gate, gate_here))):
            copies.append(pltpu.make_async_copy(source.at[here], to.at[here], arrived.at[i, shard]))
            copies[-1].start()
    x_copies = []
    for device in range(replicas):
        block = shifted(lax.axis_index("dp"), device, replicas)
        columns = pl.ds(pl.multiple_of(block * width, width), width)
        x_copies.append(pltpu.make_async_copy(x.at[:, columns], x_here[device], x_arrived.at[device]))
        x_copies[-1].start()
    for shard in range(shards):
        copies[2 * shard].wait()
        copies[2 * shard + 1].wait()
        for out, (_, cut) in zip(outs, items):
            if cut is None:
                continue
            at = out.shape[0] - hidden // LANES * shards + shard
            here = pl.ds((2 * shard + cut) * half, half)
            for column in range(hidden // LANES):
                lanes = pl.ds(column * LANES, LANES)
                g = gate_here[here, lanes].astype(F32)
                value = grad_here[here, lanes].astype(F32) * g * (0.5 + 0.5 * jnp.tanh(0.5 * g))
                out[at + column * shards] = value.astype(BF16)
    for copy in x_copies:
        copy.wait()
    for out, (of, _) in zip(outs, items):
        at = 0
        for device, cuts in of:
            for column in range(width // LANES):
                for c in cuts:
                    out[at] = x_here[device][c * half : (c + 1) * half, column * LANES : (column + 1) * LANES]
                    at += 1


def held_kernel(source, out, done):
    copy = pltpu.make_async_copy(source, out, done)
    copy.start()
    copy.wait()


def stack_kernel(places, *refs):
    *sources, out = refs
    for source, first, count, to, step in places:
        for i in range(count):
            out[to + i * step] = sources[source][first + i]


def product_kernel(shards, offsets, *refs):
    pieces, w, outs = refs[: len(offsets)], refs[len(offsets)], refs[len(offsets) + 1 :]
    columns = w.shape[1] // LANES
    bit = lax.rem(lax.axis_index("tensor"), 2)
    left = [
        jnp.concatenate([piece[at + c * shards + 2 * m + start] for c in range(columns)], axis=1)
        for start in (bit, 1 - bit)
        for piece, at in zip(pieces, offsets)
        for m in range(shards // 2)
    ]
    out = lax.dot_general(jnp.concatenate(left), w[...], NT, preferred_element_type=F32).astype(BF16)
    rows = out.shape[0] // 2
    for i, (mine, theirs) in enumerate(zip(outs[::2], outs[1::2])):
        n = rows // (len(outs) // 2)
        mine[...] = out[i * n : (i + 1) * n].reshape(mine.shape)
        theirs[...] = out[rows + i * n : rows + (i + 1) * n].reshape(theirs.shape)


def dealt_kernel(shards, offsets, rider, riders, *refs):
    pieces, w, outs = refs[: len(offsets)], refs[len(offsets)], refs[len(offsets) + 1 :]
    columns = w.shape[1] // LANES
    left = [
        jnp.concatenate([piece[at + c * shards + (lax.axis_index("tensor") ^ j)] for c in range(columns)], axis=1)
        for j in range(shards)
        for piece, at in zip(pieces, offsets)
    ]
    total = lax.dot_general(jnp.concatenate(left), w[...], NT, preferred_element_type=F32).astype(BF16)
    rows = total.shape[0] // shards
    for j, out in enumerate(outs):
        if j != rider:
            out[...] = total[j * rows : (j + 1) * rows]
            continue
        half = out.shape[1]
        for n in range(rows // half):
            for c in range(total.shape[1] // LANES):
                out[c * (rows // half) + n] = total[
                    j * rows + n * half : j * rows + (n + 1) * half, c * LANES : (c + 1) * LANES
                ]
        for piece, first, count, to, step in riders:
            for i in range(count):
                out[rows // half * (total.shape[1] // LANES) + to + i * step] = pieces[piece][first + i]


def total_kernel(count, rider, *refs):
    parts, outs = refs[:count], refs[count:]
    rows, width = parts[0].shape
    total = sum(part[...].astype(F32) for j, part in enumerate(parts) if j != rider)
    at = 0
    for out in outs:
        value = total[at : at + out.shape[0]]
        if rider is not None:
            packed = parts[rider]
            half = packed.shape[1]
            blocks = [
                jnp.concatenate(
                    [packed[c * (rows // half) + n] for c in range(width // LANES)], axis=1
                )
                for n in range(at // half, (at + out.shape[0]) // half)
            ]
            value = value + jnp.concatenate(blocks).astype(F32)
        out[...] = value.astype(BF16)
        at += out.shape[0]


def fold_kernel(step, *refs):
    *pairs, keep, give = refs
    bit = lax.rem(lax.div(lax.axis_index("tensor"), step), 2)
    at = 0
    for mine, got in zip(pairs[::2], pairs[1::2]):
        n, shards = mine.shape[:2]
        for i in range(n):
            for m in range(shards // 2):
                for to, start in ((keep, bit), (give, 1 - bit)):
                    to[at + i, m] = added(mine[i, 2 * m + start], got[i, 2 * m + start])
        at += n


def sum_kernel(mine, got, *outs):
    at = 0
    for out in outs:
        n = out.shape[0] // mine.shape[2]
        here = pl.ds(at, n)
        out[...] = added(mine[here], got[here]).reshape(out.shape)
        at += n


def crossed_kernel(mine, got, first, second, above, below):
    half = first.shape[0]
    total = added(mine[...], got[...]).reshape(-1, first.shape[1])
    above[:half], above[half:] = total[:half], second[...]
    below[:half], below[half:] = first[...], total[half:]


def weight_kernel(groups, pairs, scale, count, *refs):
    inputs, rest = refs[:count], refs[count:]
    *rest, out, right = rest
    many = 1 + max(p[0] for p in pairs)
    parts, so_far = rest[:many], rest[many:]
    half = parts[0].shape[1]
    hidden = out.shape[1]
    shards = len(groups[0])

    @pl.when(pl.program_id(0) == 0)
    def _():
        row = 0
        for part, at, _, _ in pairs:
            for j in range(shards):
                shard = lax.axis_index("tensor") ^ j
                for c in range(hidden // LANES):
                    right[pl.ds(row, half), pl.ds(c * LANES, LANES)] = parts[part][at + c * shards + shard]
                row += half

    tile = out.shape[0]
    first = pl.program_id(0) * (tile // LANES)
    left = []
    for _, _, group, at in pairs:
        for j in range(shards):
            block, start = groups[group][j]
            columns = [inputs[block][start + at + 2 * (first + c)] for c in range(tile // LANES)]
            left.append(jnp.concatenate(columns, axis=1))
    total = lax.dot_general(jnp.concatenate(left), right[...], TN, preferred_element_type=F32)
    for already in so_far:
        total += already[pl.ds(pl.multiple_of(pl.program_id(0) * tile, tile), tile)]
    out[...] = (total / scale).astype(out.dtype)


def apart_kernel(carried, out, done):
    _, _, width = out.shape
    copies = []
    for i in range(out.shape[0]):
        device = shifted(lax.axis_index("dp"), i + 1, out.shape[0] + 1)
        columns = pl.ds(pl.multiple_of(device * width, width), width)
        copies.append(pltpu.make_async_copy(carried.at[:, columns], out.at[i], done.at[i]))
        copies[-1].start()
    for copy in copies:
        copy.wait()


def merged_kernel(carried, piece, out):
    width = piece.shape[1]
    columns = pl.ds(pl.multiple_of(lax.axis_index("dp") * width, width), width)
    out[...] = added(carried[:, columns], piece[...])


def first_kernel(piece, out, total, done):
    width = piece.shape[1]
    columns = pl.ds(pl.multiple_of(lax.axis_index("dp") * width, width), width)
    sent = lax.axis_index("section") < lax.axis_size("section") - 1
    total[...] = jnp.where(sent, piece[...], jnp.zeros(piece.shape, BF16))
    copy = pltpu.make_async_copy(total, out.at[:, columns], done)
    copy.start()
    copy.wait()


def last_kernel(blocks, base, *refs):
    *pieces, _, out, total, done = refs
    width = pieces[0].shape[1]
    replicas = base.shape[0] + 1
    sent = lax.axis_index("section") < lax.axis_size("section") - 1
    copies = []
    for i, (block, piece) in enumerate(zip(blocks, pieces)):
        device = shifted(lax.axis_index("dp"), block, replicas)
        columns = pl.ds(pl.multiple_of(device * width, width), width)
        total[i] = jnp.where(sent, added(base[block - 1], piece[...]), jnp.zeros(piece.shape, BF16))
        copies.append(pltpu.make_async_copy(total.at[i], out.at[:, columns], done.at[i]))
        copies[-1].start()
    for copy in copies:
        copy.wait()


def body(section_input, carried_grad, hidden_grad, saved_gate, w_up):
    sizes = tuple(lax.axis_size(a) for a in AXES)
    sections, replicas, shards = sizes
    grad, gate, x = hidden_grad[0, 0], saved_gate[0, 0], section_input[0, 0]
    w = w_up[0]
    width, hidden = w.shape
    tokens, rows = grad.shape[0], x.shape[0]
    half = rows // 2
    last, middle = replicas - 1, replicas // 2
    up_count, x_count = hidden // LANES * shards, width // LANES

    def up(value):
        return moved(value, sizes, lambda s, i, j: (s, shifted(i, 1, replicas), j))

    def down(value):
        return moved(value, sizes, lambda s, i, j: (s, shifted(i, -1, replicas), j))

    def returned(value, k):
        return moved(
            value,
            sizes,
            lambda s, i, j: (s - 1, shifted(i, -k, replicas), j) if s else (sections - 1, i, j),
        )

    def across(value, step):
        return moved(value, sizes, lambda s, i, j: (s, i, j ^ step))

    def product(*pieces, groups=1, flops=0):
        share = (len(pieces) // groups, shards // 2, half, width)
        kernel = functools.partial(product_kernel, shards, [at for _, at in pieces])
        return call(kernel, [share] * (2 * groups), *[piece for piece, _ in pieces], w, flops=flops)

    def summed(pieces, halves, rider=None, riders=()):
        kernel = functools.partial(dealt_kernel, shards, [at for _, at in pieces], rider, riders)
        shares = [(len(pieces) * half, width)] * shards
        own = len(pieces) * x_count
        if rider is not None:
            shares[rider] = (own + sum(count for _, _, count, _, _ in riders), half, LANES)
        mine, *others = call(kernel, shares, *[piece for piece, _ in pieces], w)
        others = [across(v, j + 1) for j, v in enumerate(others)]
        kernel = functools.partial(total_kernel, shards, rider)
        outs = call(kernel, [(n * half, width) for n in halves], mine, *others)
        return outs, others[rider - 1] if rider is not None else None

    def fold(step, *pairs):
        n, m = sum(v.shape[0] for v in pairs[::2]), pairs[0].shape[1]
        share = (n, m // 2, half, width)
        return call(functools.partial(fold_kernel, step), [share, share], *pairs)

    def finished(mine, got, *halves):
        step = 4
        while step < shards:
            mine, give = fold(step, mine, got)
            got = across(give, step)
            step *= 2
        return call(sum_kernel, [(n * half, width) for n in halves], mine, got)

    def stacked(count, places, *sources):
        return call(functools.partial(stack_kernel, places), [(count, half, LANES)], *sources)[0]

    def doubled(block, step, steps):
        for _ in range(steps):
            n = block.shape[0]
            places = [(i, 0, n, i * n, 1) for i in range(2)]
            block = stacked(2 * n, places, block, across(block, step))
            step //= 2
        return block

    far_step, steps = shards // 2, shards.bit_length() - 1
    order = [0]
    for i in range(steps - 1):
        order += [j + (far_step >> i) for j in order]

    tile = 512

    def weight_product(xs, pairs, parts, *so_far, final):
        groups, at = [], 0
        for x in xs:
            group = [None] * shards
            for i, j in enumerate(order):
                for other in (0, 1):
                    if len(x) == 2:
                        group[j ^ other] = (at + other, i * (x[0].shape[0] // len(order)))
                    else:
                        group[j ^ other] = (at + (j ^ other), 0)
            groups.append(group)
            at += len(x)
        kernel = functools.partial(weight_kernel, groups, pairs, replicas if final else 1, at)
        return call(
            kernel,
            [jax.ShapeDtypeStruct((width, hidden), BF16 if final else F32)],
            *[v for x in xs for v in x],
            *parts,
            *so_far,
            grid=(width // tile,),
            out_specs=[pl.BlockSpec((tile, hidden), lambda i: (i, 0))],
            scratch_shapes=[pltpu.VMEM((len(pairs) * shards * half, hidden), BF16)],
            limit=20,
        )[0]

    both = (0, 1)
    items = [[(d, both) for d in range(1, (replicas + 1) // 2)], [(last + 1 - d, both) for d in range(1, (replicas + 1) // 2)]]
    if replicas % 2 == 0:
        for cut in both:
            items[cut].append((middle, (cut,)))
    items = [(items[0], 0), (items[1], 1), ([(0, both)], None)]
    counts = [sum(x_count * len(cuts) for _, cuts in of) + (cut is not None) * up_count for of, cut in items]
    a, b, x_own = call(
        functools.partial(start_kernel, shards, items),
        [(n, half, LANES) for n in counts],
        grad,
        gate,
        x,
        in_specs=[HBM] * 3,
        scratch_shapes=[pltpu.VMEM((tokens, hidden), BF16)] * 2
        + [[pltpu.VMEM((rows, width), BF16)] * replicas]
        + [pltpu.SemaphoreType.DMA((2, shards)), pltpu.SemaphoreType.DMA((replicas,))],
        limit=START,
    )
    a_next, b_next = up(a), down(b)
    carried, *_ = together(carried_grad[0, 0], a, b)
    base = call(
        apart_kernel,
        [(last, rows, width)],
        carried,
        in_specs=[HBM],
        scratch_shapes=[pltpu.SemaphoreType.DMA((last,))],
    )[0]
    base = returned(base, 0)
    w = call(held_kernel, [w.shape], w, in_specs=[HBM], scratch_shapes=[pltpu.SemaphoreType.DMA])[0]
    at = a.shape[0] - up_count
    a_parts, b_parts, ats = [a], [b], [at]
    (out,), _ = summed([(a, at), (b, at)], [2])
    x_own = doubled(x_own, far_step, steps - 1)
    x_own = [x_own, across(x_own, 1)]

    a, b, base, out, *x_own = together(a_next, b_next, base, out, *x_own)
    a_parts.append(a)
    b_parts.append(b)
    ats.append(at)
    a_next, b_next = up(a[2 * x_count :]), down(b[2 * x_count :])
    zero = returned(call(merged_kernel, [(rows, width)], carried_grad[0, 0], out)[0], 0)
    keep_a, give_a, keep_b, give_b = product((a, at), (b, at), groups=2)
    keep, give = fold(2, keep_a, across(give_a, 1), keep_b, across(give_b, 1))
    nears = finished(keep, across(give, 2), 1, 1)
    x_near = stacked(4 * x_count, [(i, 0, 2 * x_count, 2 * i * x_count, 1) for i in range(2)], a, b)
    x_near, step = {0: x_near}, far_step
    while step > 1:
        x_near |= {j + step: across(v, step) for j, v in x_near.items()}
        step //= 2
    blocks = sorted(x_near)
    x_near = [x_near[j] for j in blocks]

    at -= 2 * x_count
    weight_grad = weight_product(
        [x_own], [(0, ats[0], 0, 0), (1, ats[0], 0, 1)], [a_parts[0], b_parts[0]], final=False
    )
    a, b, zero, weight_grad, *nears = together(a_next, b_next, zero, weight_grad, *nears)
    a_parts.append(a)
    b_parts.append(b)
    ats.append(at)
    a_next, b_next = up(a[x_count:]), down(b[x_count:])
    far_a, far_b, *x_near = together(a, b, *x_near)
    riders = [(i, 0, x_count, i, 2) for i in range(2)]
    (out,), x_far = summed([(far_a, at), (far_b, at)], [2], far_step, riders)

    at -= x_count
    a, b = a_next, b_next
    a_parts.append(a)
    b_parts.append(b)
    ats.append(at)
    keep, give = product((a, at), (b, at), flops=2 * tokens * hidden * width)
    passed = call(
        first_kernel,
        [(rows, replicas * width)],
        zero,
        out_specs=[HBM],
        scratch_shapes=[pltpu.VMEM((rows, width), BF16), pltpu.SemaphoreType.DMA],
    )[0]
    x_far, give, out, passed = together(x_far, give, out, passed)
    keep, give = fold(2, keep, across(give, 1))
    got = across(give, 2)
    out, _ = together(out, give)
    two = returned(out, 0)
    x_near = [v for pair in ((v, across(v, 1)) for v in x_near) for v in pair]
    places = [(i, 0, x_count, i, 2) for i in range(2)] + [(2, 2 * x_count, 2 * x_count, 2 * x_count, 1)]
    x_far = stacked(4 * x_count, places, a_parts[2], b_parts[2], x_far)
    x_far = doubled(x_far, far_step // 2, steps - 2)
    x_far = [x_far, across(x_far, 1)]

    parts = [v for pair_of in zip(a_parts, b_parts) for v in pair_of]
    step = 4
    while step < shards:
        keep, give = fold(step, keep, got)
        got = across(give, step)
        step *= 2
    above, below = call(crossed_kernel, [(rows, width)] * 2, keep, got, *nears)
    out = above
    above, below = returned(above, -1), returned(below, 1)
    two = moved(
        two, sizes, lambda s, i, j: (s, shifted(i, -2, replicas), j) if s < sections - 1 else (s, i, j ^ 1)
    )

    weight_grad, _ = together(weight_grad, out)
    weight_grad = weight_product(
        [x_near, x_far],
        [
            (0, ats[1], 0, 0),
            (1, ats[1], 0, 2 * x_count + 1),
            (2, ats[2], 1, 0),
            (3, ats[2], 1, 1),
            (4, ats[3], 0, 2 * x_count),
            (5, ats[3], 0, 1),
        ],
        parts[2:],
        weight_grad,
        final=True,
    )
    passed, weight_grad = together(passed, weight_grad)
    passed, above, below = together(passed, above, below)
    passed = call(
        functools.partial(last_kernel, [2, last, 1]),
        [passed.shape],
        base,
        two,
        above,
        below,
        passed,
        in_specs=[VMEM] * 4 + [HBM],
        out_specs=[HBM],
        scratch_shapes=[pltpu.VMEM((3, rows, width), BF16), pltpu.SemaphoreType.DMA((3,))],
        input_output_aliases={4: 0},
    )[0]
    return passed[None, None], weight_grad[None]


def solution(mesh):
    return jax.shard_map(
        body,
        mesh=mesh,
        in_specs=(
            P("section", "dp", "tensor", None),
            P("section", "dp", "tensor", None),
            P("section", "dp", None, "tensor"),
            P("section", "dp", None, "tensor"),
            P("section", "dp", "tensor"),
        ),
        out_specs=(P("section", "dp", "tensor", None), P("section", "dp", "tensor")),
        check_vma=False,
    )
```
